32 devices in a mesh: ctx: 8 (over z, x), head: 4 (over y, core).
Axes of the slice: x: 2, y: 2, z: 4, core: 2. Of those that a mesh axis runs over, the one named last changes fastest.
Arguments:
- head_input: float32 [2048, 1024], P('ctx', 'head'), may hold values from -6 to 6
- step_size: float32 [16, 2048], P('head', 'ctx'), may hold values from 0.25 to 2
- log_decay: float32 [16, 2048], P('head', 'ctx'), may hold values from -1.6 to 0
- write_proj: float32 [2048, 128], P('ctx'), may hold values from -1.0606601 to 1.0606601
- read_proj: float32 [2048, 128], P('ctx'), may hold values from -0.5 to 0.5
- grad_out: float32 [2048, 1024], P('ctx', 'head'), may hold values from -6 to 6
Outputs:
- head_output: float32 [2048, 1024], P('ctx', 'head')
- grad_input: float32 [2048, 1024], P('ctx', 'head')
- grad_step: float32 [16, 2048], P('head', 'ctx')
- write_grad: float32 [2048, 128], P(('ctx', 'head'))
- read_grad: float32 [2048, 128], P(('ctx', 'head'))
The draws below stay inside these ranges and needn't reach their ends.
All inputs are finite; a program needn't handle non-finite values.
Results may differ from the reference program's by a relative error of at most 0.00022.
Values sent between devices are 32-bit elements; how exact they have to be, the bound alone decides.
A program may use at most 64 MiB of HBM per device.

```python
import math
import jax
import jax.numpy as jnp
from jax import lax

HEAD_DIM = 64
STATE = 128
GROUP = 128
TOK_DEV = 256
HEADS = 16
SEQUENCE_TOKENS = 2048


def draw_log_decay(key, part):
    random_keys = jax.random.split(key, 7)
    fast_share = 0.5
    chosen = jax.random.uniform(random_keys[0], (HEADS, 1), dtype=jnp.float32)
    fast_rate = 1.0 / 40.0 * jnp.exp(jax.random.uniform(random_keys[1], (HEADS, 1), dtype=jnp.float32, minval=-0.29, maxval=0.29))
    slow_rate = 0.25 / SEQUENCE_TOKENS * jnp.exp(jax.random.uniform(random_keys[2], (HEADS, 1), dtype=jnp.float32, minval=-0.69, maxval=0.69))
    selected_rate = jnp.where(chosen < fast_share, fast_rate, slow_rate)
    jaggedness = jnp.exp(jax.random.uniform(random_keys[3], (HEADS, SEQUENCE_TOKENS), dtype=jnp.float32, minval=-0.69, maxval=0.69))
    block_count = SEQUENCE_TOKENS // TOK_DEV
    block_multiplier = jnp.exp(jax.random.uniform(random_keys[4], (HEADS, block_count, 1), dtype=jnp.float32, minval=-0.69, maxval=0.69))
    block_multiplier = jnp.broadcast_to(block_multiplier, (HEADS, block_count, TOK_DEV)).reshape(HEADS, SEQUENCE_TOKENS)
    spike_positions = jax.random.randint(random_keys[5], (3,), 0, SEQUENCE_TOKENS)
    spike_depth = jax.random.uniform(random_keys[6], (3,), dtype=jnp.float32, minval=0.22, maxval=0.69)
    spike_locations = (jnp.arange(SEQUENCE_TOKENS)[None, :] == spike_positions[:, None]).astype(jnp.float32)
    spike_count = jnp.sum(spike_locations * spike_depth[:, None], axis=0)
    return -(selected_rate * jaggedness * block_multiplier) - spike_count[None, :]


def levels(rng, extent, cuts, smallest, largest):
    def one(axis_at, shards_of):
        heights = jax.random.uniform(jax.random.fold_in(jax.random.fold_in(rng, 6), axis_at), (shards_of,), jnp.float32, smallest / len(cuts), largest / len(cuts))
        return jnp.repeat(jnp.exp(heights), extent[axis_at] // shards_of).reshape((-1,) + (1,) * (len(extent) - axis_at - 1))

    gain = one(*cuts[0])
    for cut in cuts[1:]:
        gain = gain * one(*cut)
    return gain


def centred(key, extent, width, reach, shards=(), kind=jnp.bfloat16):
    result = jax.random.normal(key, extent, jnp.float32) * width
    if len(shards) > 0:
        result = levels(key, extent, shards, -0.22, 0.18) * result
    return jnp.clip(result, min=-reach, max=reach).astype(kind)


def setup_inputs(seed: int = 0) -> dict:
    arg_keys = jax.random.split(jax.random.key(seed), 7)
    head_input = centred(arg_keys[0], (SEQUENCE_TOKENS, HEADS * HEAD_DIM), 1.0, 6.0, ((0, 8), (1, 4)), jnp.float32)
    step_size = jnp.clip(jnp.exp(math.log(2.0) - 2.0794415 * jax.random.uniform(arg_keys[1], (HEADS, SEQUENCE_TOKENS), jnp.float32) ** levels(arg_keys[1], (HEADS, SEQUENCE_TOKENS), ((0, 4), (1, 8)), -0.2, 0.2)), 0.25, 2.0)
    log_decay = draw_log_decay(jax.random.fold_in(arg_keys[6], 71), 0)
    write_proj = centred(arg_keys[3], (SEQUENCE_TOKENS, STATE), ((SEQUENCE_TOKENS // 64) ** -0.5), 1.0606601, ((0, 8),), jnp.float32)
    read_proj = centred(arg_keys[4], (SEQUENCE_TOKENS, STATE), STATE ** -0.5, 0.5, ((0, 8),), jnp.float32)
    grad_out = centred(arg_keys[5], (SEQUENCE_TOKENS, HEADS * HEAD_DIM), 1.0, 6.0, ((0, 8), (1, 4)), jnp.float32)
    return dict(head_input=head_input, step_size=step_size, log_decay=log_decay, write_proj=write_proj, read_proj=read_proj, grad_out=grad_out)


def group_step(carry_state, piece):
    scaled_part, rate_part, write_part, read_part = piece
    highest = lax.Precision.HIGHEST
    cumulated = jnp.cumsum(rate_part, axis=1)
    lower_mask = jnp.tril(jnp.ones((GROUP, GROUP), dtype=bool))
    gap_logs = cumulated[:, :, None] - cumulated[:, None, :]
    decay_mat = jnp.where(lower_mask[None], jnp.exp(jnp.where(lower_mask[None], gap_logs, 0.0)), 0.0)
    inner_prod = jnp.dot(read_part, write_part.T, precision=highest)
    local_term = jnp.einsum('hts,shp->thp', inner_prod[None] * decay_mat, scaled_part, precision=highest)
    carried_term = jnp.einsum('tn,hnp->thp', read_part, carry_state, precision=highest)
    result_rows = local_term + jnp.exp(cumulated).T[:, :, None] * carried_term
    final_cum = cumulated[:, -1:]
    weighted = jnp.exp(final_cum - cumulated).T[:, :, None] * scaled_part
    update_term = jnp.einsum('sn,shp->hnp', write_part, weighted, precision=highest)
    new_state = jnp.exp(final_cum)[:, :, None] * carry_state + update_term
    return (new_state, result_rows)

def forward(head_input, step_size, write_proj, read_proj, log_decay):
    num_groups = SEQUENCE_TOKENS // GROUP
    scaled = head_input.reshape(SEQUENCE_TOKENS, HEADS, HEAD_DIM) * step_size.T[:, :, None]
    scaled = scaled.reshape(num_groups, GROUP, HEADS, HEAD_DIM)
    group_rates = log_decay.reshape(HEADS, num_groups, GROUP).transpose(1, 0, 2)
    write_parts = write_proj.reshape(num_groups, GROUP, STATE)
    read_parts = read_proj.reshape(num_groups, GROUP, STATE)
    zero_state = jnp.zeros((HEADS, STATE, HEAD_DIM), dtype=jnp.float32)
    final_state, group_results = lax.scan(jax.checkpoint(group_step), zero_state, (scaled, group_rates, write_parts, read_parts))
    return group_results.reshape(SEQUENCE_TOKENS, HEADS * HEAD_DIM)

def reference(head_input, step_size, log_decay, write_proj, read_proj, grad_out):

    def applied(input_val, step_val, write_val, read_val):
        return forward(input_val, step_val, write_val, read_val, log_decay)
    head_output, pullback = jax.vjp(applied, head_input, step_size, write_proj, read_proj)
    grad_input, grad_step, write_grad, read_grad = pullback(grad_out)
    return (head_output, grad_input, grad_step, write_grad, read_grad)
```

```python
import functools

import jax
import jax.numpy as jnp
from jax import lax
from jax.experimental import pallas as pl
from jax.experimental.pallas import tpu as pltpu
from jax.sharding import PartitionSpec as P

MESH = pl.DeviceIdType.MESH
F32 = jnp.float32
BF16 = jnp.bfloat16
HIGHEST = lax.Precision.HIGHEST
PAD = 8


def split(x):
    high = x.astype(BF16)
    return high, (x - high.astype(F32)).astype(BF16)


def dot3(a, b, ca, cb):
    dims = (((ca,), (cb,)), ((), ()))
    dot = functools.partial(lax.dot_general, dimension_numbers=dims, preferred_element_type=F32)
    return dot(a[0], b[0]) + (dot(a[0], b[1]) + dot(a[1], b[0]))


def exact(a, b, ca, cb):
    dims = (((ca,), (cb,)), ((), ()))
    return lax.dot_general(a, b, dims, precision=HIGHEST, preferred_element_type=F32)


def kernel(
    n, nh,
    x_ref, step_ref, log_ref, b_ref, c_ref, g_ref,
    out_ref, gin_ref, gstep_ref, wg_ref, rg_ref,
    st, r1, tz, zbuf, fsend, fs, tot, rs, wsum, back,
    s1_send, s1_recv, z_send, z_recv, s3_send, s3_recv, h_send, h_recv,
):
    tokens, channels = x_ref.shape
    heads = step_ref.shape[0]
    width = channels // heads
    state = b_ref.shape[1]
    half = channels // 2
    half_heads = heads // 2
    m = n // 2
    ck = tokens // nh

    ctx, head = lax.axis_index("ctx"), lax.axis_index("head")
    side, row = lax.rem(ctx, 2), lax.div(ctx, 2)
    partner = row * 2 + (1 - side)

    barrier = pltpu.get_barrier_semaphore()
    pl.semaphore_signal(barrier, inc=1, device_id=(partner, head), device_id_type=MESH)
    for k in range(1, m):
        peer = lax.rem(row + k, m) * 2 + side
        pl.semaphore_signal(barrier, inc=1, device_id=(peer, head), device_id_type=MESH)
    for k in range(1, nh):
        pl.semaphore_signal(
            barrier, inc=1, device_id=(ctx, lax.rem(head + k, nh)), device_id_type=MESH
        )

    mid = tokens // 2
    t_ids = lax.broadcasted_iota(jnp.int32, (tokens, tokens), 0)
    s_ids = lax.broadcasted_iota(jnp.int32, (tokens, tokens), 1)
    lower = t_ids >= s_ids
    weights = jnp.where(
        lower & (s_ids >= mid), 1.0, jnp.where((s_ids > t_ids) & (s_ids < mid), -1.0, 0.0)
    ).astype(F32)
    logs = log_ref[...]
    rel = exact(logs, weights, 1, 1)
    before = jnp.sum(logs[:, :mid], axis=1, keepdims=True)
    last = rel[:, tokens - 1 : tokens]
    into = jnp.exp(rel + before)
    outof = jnp.exp(last - rel)
    total = jnp.exp(last + before)
    cols = jnp.concatenate([step_ref[...], into, outof, rel], axis=0).T
    pick_row = lax.broadcasted_iota(jnp.int32, (4 * heads, 3 * channels), 0)
    pick_col = lax.broadcasted_iota(jnp.int32, (4 * heads, 3 * channels), 1)
    expand = (pick_col // width == pick_row).astype(F32)
    wide = exact(cols, expand, 1, 0)
    step_w = wide[:, :channels]
    into_w = wide[:, channels : 2 * channels]
    outof_w = wide[:, 2 * channels :]

    grads = g_ref[...]
    scaled = x_ref[...] * step_w
    into_g = split(into_w * grads)
    outof_s = split(outof_w * scaled)
    write, read = split(b_ref[...]), split(c_ref[...])
    fwd = dot3(outof_s, write, 0, 0)
    bwd = dot3(into_g, read, 0, 0)
    for j in range(2):
        decay_rows = jnp.broadcast_to(
            total[j * half_heads : (j + 1) * half_heads], (half_heads, state)
        )
        decay_rows = jnp.concatenate([decay_rows] * (PAD // half_heads), axis=0)
        for d, whole in enumerate((fwd, bwd)):
            st[j, d, :half] = whole[j * half : (j + 1) * half]
            st[j, d, half:] = decay_rows

    def widen(rows):
        return jnp.concatenate(
            [jnp.broadcast_to(rows[i : i + 1], (width, state)) for i in range(half_heads)], axis=0
        )

    pl.semaphore_wait(barrier, 1 + (m - 1) + (nh - 1))
    first_copy = pltpu.make_async_remote_copy(
        st.at[1 - side], r1, s1_send, s1_recv, device_id=(partner, head), device_id_type=MESH
    )
    first_copy.start()

    scaled_2, grads_2 = split(scaled), split(grads)
    inner = dot3(read, write, 1, 1)
    lane = lax.broadcasted_iota(jnp.int32, (tokens, channels), 1) // width

    def near(h):
        gap = cols[:, 3 * heads + h : 3 * heads + h + 1] - rel[h : h + 1, :]
        decay = jnp.where(lower, jnp.exp(jnp.where(lower, gap, 0.0)), 0.0)
        mixed = split(inner * decay)
        mine = lane == h

        def only(pair):
            return tuple(jnp.where(mine, part.astype(F32), 0.0).astype(BF16) for part in pair)

        scaled_h, grads_h = only(scaled_2), only(grads_2)
        out_h = dot3(mixed, scaled_h, 1, 0)
        back_h = dot3(mixed, grads_h, 0, 0)
        pair_h = decay * dot3(grads_2, scaled_h, 1, 1)
        if h == 0:
            out_ref[...] = out_h
            back[...] = back_h
            wsum[...] = pair_h
        else:
            out_ref[...] += out_h
            back[...] += back_h
            wsum[...] += pair_h

    near(0)
    first_copy.wait()

    own, other = st[side], r1[...]
    is_first = side == 0
    part_0 = jnp.where(is_first, own, other)
    part_1 = jnp.where(is_first, other, own)
    decay_0, decay_1 = part_0[0, half:], part_1[0, half:]
    wide_0, wide_1 = widen(decay_0), widen(decay_1)
    fwd_0, fwd_1 = part_0[0, :half], part_1[0, :half]
    bwd_0, bwd_1 = part_0[1, :half], part_1[1, :half]
    tz[0, :half] = wide_1 * fwd_0 + fwd_1
    tz[1, :half] = bwd_0 + wide_0 * bwd_1
    for d in range(2):
        tz[d, half:] = decay_0 * decay_1

    z_copies = []
    for k in range(1, m):
        peer_row = lax.rem(row + k, m)
        direction = jnp.where(peer_row > row, 0, 1)
        copy = pltpu.make_async_remote_copy(
            tz.at[direction], zbuf.at[row], z_send.at[k - 1], z_recv.at[row],
            device_id=(peer_row * 2 + side, head), device_id_type=MESH,
        )
        copy.start()
        z_copies.append(copy)

    for h in range(1, heads - 1):
        near(h)

    def joined(j, carried):
        pltpu.make_async_remote_copy(
            tz.at[0], zbuf.at[j], z_send.at[0], z_recv.at[j],
            device_id=(partner, head), device_id_type=MESH,
        ).wait_recv()
        arrived = zbuf[j]
        return arrived[:half] + widen(arrived[half:]) * carried

    zero = jnp.zeros((half, state), F32)
    carry_f = lax.fori_loop(0, row, joined, zero)
    carry_b = lax.fori_loop(0, m - 1 - row, lambda i, c: joined(m - 1 - i, c), zero)

    enter_f = (carry_f, wide_0 * carry_f + fwd_0)
    enter_b = (bwd_1 + wide_1 * carry_b, carry_b)
    for d, pair in enumerate((enter_f, enter_b)):
        fs[side, d] = jnp.where(is_first, pair[0], pair[1])
        fsend[d] = jnp.where(is_first, pair[1], pair[0])
    last_copy = pltpu.make_async_remote_copy(
        fsend, fs.at[side], s3_send, s3_recv, device_id=(partner, head), device_id_type=MESH
    )
    last_copy.start()

    near(heads - 1)
    sums = split(wsum[...])
    read_near = dot3(sums, write, 1, 0)
    write_near = dot3(sums, read, 0, 0)
    last_copy.wait()

    state_f = split(jnp.concatenate([fs[0, 0], fs[1, 0]], axis=0))
    state_b = split(jnp.concatenate([fs[0, 1], fs[1, 1]], axis=0))
    write_all = write_near + dot3(outof_s, state_b, 1, 0)
    read_all = read_near + dot3(into_g, state_f, 1, 0)
    for j in range(nh):
        tot[j, :ck] = write_all[j * ck : (j + 1) * ck]
        tot[j, ck:] = read_all[j * ck : (j + 1) * ck]
    h_copies = []
    for k in range(1, nh):
        peer = lax.rem(head + k, nh)
        copy = pltpu.make_async_remote_copy(
            tot.at[peer], rs.at[k - 1], h_send.at[k - 1], h_recv.at[k - 1],
            device_id=(ctx, peer), device_id_type=MESH,
        )
        copy.start()
        h_copies.append(copy)

    out_ref[...] += into_w * dot3(read, state_f, 1, 1)
    back_all = back[...] + outof_w * dot3(write, state_b, 1, 1)
    gin_ref[...] = step_w * back_all
    sum_row = lax.broadcasted_iota(jnp.int32, (heads, channels), 0)
    sum_col = lax.broadcasted_iota(jnp.int32, (heads, channels), 1)
    gstep_ref[...] = exact((sum_col // width == sum_row).astype(F32), x_ref[...] * back_all, 1, 1)

    result = tot[head]
    for k, copy in enumerate(h_copies):
        copy.wait()
        result = result + rs[k]
    wg_ref[...] = result[:ck]
    rg_ref[...] = result[ck:]
    for copy in z_copies:
        copy.wait_send()


def solution(mesh):
    n, nh = mesh.shape["ctx"], mesh.shape["head"]
    m = n // 2

    def shards(head_input, step_size, log_decay, write_proj, read_proj, grad_out):
        tokens, channels = head_input.shape
        heads = step_size.shape[0]
        state = write_proj.shape[1]
        half, ck = channels // 2, tokens // nh
        vmem = pl.BlockSpec(memory_space=pltpu.VMEM)
        dma = pltpu.SemaphoreType.DMA
        return pl.pallas_call(
            functools.partial(kernel, n, nh),
            out_shape=(
                jax.ShapeDtypeStruct((tokens, channels), F32),
                jax.ShapeDtypeStruct((tokens, channels), F32),
                jax.ShapeDtypeStruct((heads, tokens), F32),
                jax.ShapeDtypeStruct((ck, state), F32),
                jax.ShapeDtypeStruct((ck, state), F32),
            ),
            in_specs=[vmem] * 6,
            out_specs=(vmem,) * 5,
            scratch_shapes=[
                pltpu.VMEM((2, 2, half + PAD, state), F32),
                pltpu.VMEM((2, half + PAD, state), F32),
                pltpu.VMEM((2, half + PAD, state), F32),
                pltpu.VMEM((m, half + PAD, state), F32),
                pltpu.VMEM((2, half, state), F32),
                pltpu.VMEM((2, 2, half, state), F32),
                pltpu.VMEM((nh, 2 * ck, state), F32),
                pltpu.VMEM((nh - 1, 2 * ck, state), F32),
                pltpu.VMEM((tokens, tokens), F32),
                pltpu.VMEM((tokens, channels), F32),
                dma, dma, dma((m - 1,)), dma((m,)), dma, dma, dma((nh - 1,)), dma((nh - 1,)),
            ],
            compiler_params=pltpu.CompilerParams(
                collective_id=0, has_side_effects=True, vmem_limit_bytes=40 * 2**20
            ),
        )(head_input, step_size, log_decay, write_proj, read_proj, grad_out)

    return jax.shard_map(
        shards,
        mesh=mesh,
        in_specs=(
            P("ctx", "head"), P("head", "ctx"), P("head", "ctx"),
            P("ctx", None), P("ctx", None), P("ctx", "head"),
        ),
        out_specs=(
            P("ctx", "head"), P("ctx", "head"), P("head", "ctx"),
            P(("ctx", "head"), None), P(("ctx", "head"), None),
        ),
        check_vma=False,
    )
```

```python
import functools

import jax
import jax.numpy as jnp
from jax import lax
from jax.experimental import pallas as pl
from jax.experimental.pallas import tpu as pltpu
from jax.sharding import PartitionSpec as P

MESH = pl.DeviceIdType.MESH
F32 = jnp.float32
BF16 = jnp.bfloat16
PAD = 8
GRANT = 60 * 2**20
CHUNKS = 2


def split(x):
    high = x.astype(BF16)
    return high, (x - high.astype(F32)).astype(BF16)


def dot3(a, b, ca, cb):
    dims = (((ca,), (cb,)), ((), ()))
    dot = functools.partial(lax.dot_general, dimension_numbers=dims, preferred_element_type=F32)
    return dot(a[0], b[0]) + (dot(a[0], b[1]) + dot(a[1], b[0]))


def thirds(rows):
    zeros = jnp.zeros((16 - rows.shape[0], rows.shape[1]), F32)
    pieces = []
    for _ in range(3):
        piece = rows.astype(BF16)
        rows = rows - piece.astype(F32)
        pieces.append(jnp.concatenate([piece.astype(F32), zeros], axis=0))
    return jnp.concatenate(pieces, axis=0).astype(BF16)


def kernel(
    n, nh,
    x_hbm, step_hbm, log_hbm, b_hbm, c_hbm, g_hbm,
    out_hbm, gin_hbm, gstep_hbm, wg_hbm, rg_hbm,
    x_ref, step_ref, log_ref, b_ref, c_ref, g_ref,
    out_ref, gin_ref, gstep_ref, wg_ref, rg_ref,
    st, r1, tz, zbuf, fsend, fs, tot, rs, wsum, back,
    in_sem, out_sem, s1_send, s1_recv, z_send, z_recv, s3_send, s3_recv, h_send, h_recv,
):
    tokens, channels = x_ref.shape
    heads = step_ref.shape[0]
    width = channels // heads
    state = b_ref.shape[1]
    half = channels // 2
    m = n // 2
    ck = tokens // nh
    piece = state // CHUNKS

    ctx, head = lax.axis_index("ctx"), lax.axis_index("head")
    side, row = lax.rem(ctx, 2), lax.div(ctx, 2)
    partner = row * 2 + (1 - side)

    barrier = pltpu.get_barrier_semaphore()
    pl.semaphore_signal(barrier, inc=1, device_id=(partner, head), device_id_type=MESH)
    for k in range(1, m):
        peer = lax.rem(row + k, m) * 2 + side
        pl.semaphore_signal(barrier, inc=1, device_id=(peer, head), device_id_type=MESH)
    for k in range(1, nh):
        pl.semaphore_signal(
            barrier, inc=1, device_id=(ctx, lax.rem(head + k, nh)), device_id_type=MESH
        )

    loads = [
        pltpu.make_async_copy(source, target, in_sem.at[i])
        for i, (source, target) in enumerate((
            (log_hbm, log_ref), (step_hbm, step_ref), (b_hbm, b_ref),
            (c_hbm, c_ref), (x_hbm, x_ref), (g_hbm, g_ref),
        ))
    ]
    for load in loads:
        load.start()

    stores = [
        pltpu.make_async_copy(source, target, out_sem.at[i])
        for i, (source, target) in enumerate((
            (out_ref, out_hbm), (gin_ref, gin_hbm), (gstep_ref, gstep_hbm),
            (wg_ref, wg_hbm), (rg_ref, rg_hbm),
        ))
    ]

    mid = tokens // 2
    row_ids = lax.broadcasted_iota(jnp.int32, (tokens, tokens), 0)
    col_ids = lax.broadcasted_iota(jnp.int32, (tokens, tokens), 1)
    weights = jnp.where(
        (row_ids <= col_ids) & (row_ids >= mid),
        1.0,
        jnp.where((row_ids > col_ids) & (row_ids < mid), -1.0, 0.0),
    ).astype(BF16)
    pick_row = lax.broadcasted_iota(jnp.int32, (48, 3 * channels), 0) % 16
    pick_col = lax.broadcasted_iota(jnp.int32, (48, 3 * channels), 1) // width
    expand = jnp.where(pick_row == pick_col, 1.0, 0.0).astype(BF16)

    loads[0].wait()
    logs = log_ref[...]
    sums = jnp.dot(thirds(logs), weights, preferred_element_type=F32)
    rel = sums[:heads] + sums[16 : 16 + heads] + sums[32 : 32 + heads]
    before = jnp.sum(logs[:, :mid], axis=1, keepdims=True)
    last = rel[:, tokens - 1 : tokens]
    into = jnp.exp(rel + before)
    outof = jnp.exp(last - rel)
    loads[1].wait()
    factors = thirds(jnp.concatenate([step_ref[...], into, outof], axis=0))
    wide = lax.dot_general(
        factors, expand, (((0,), (0,)), ((), ())), preferred_element_type=F32
    )
    step_w = wide[:, :channels]
    into_w = wide[:, channels : 2 * channels]
    outof_w = wide[:, 2 * channels :]

    loads[2].wait()
    write, write_t = split(b_ref[...]), split(b_ref[...].T)
    loads[3].wait()
    read, read_t = split(c_ref[...]), split(c_ref[...].T)
    loads[4].wait()
    scaled = x_ref[...] * step_w
    outof_s = split(outof_w * scaled)
    fwd = dot3(write_t, outof_s, 1, 0)
    loads[5].wait()
    grads = g_ref[...]
    into_g = split(into_w * grads)
    bwd = dot3(read_t, into_g, 1, 0)
    decay_rows = jnp.broadcast_to(into_w[tokens - 1 : tokens], (PAD, channels))
    for j in range(2):
        for d, whole in enumerate((fwd, bwd)):
            st[j, d, :PAD] = decay_rows[:, j * half : (j + 1) * half]
            st[j, d, PAD:] = whole[:, j * half : (j + 1) * half]

    def span(i):
        return pl.ds(0, PAD + piece) if i == 0 else pl.ds(PAD + i * piece, piece)

    def spread(decay):
        return jnp.concatenate([decay] * (piece // PAD), axis=0)

    pl.semaphore_wait(barrier, 1 + (m - 1) + (nh - 1))
    first_copies = [
        pltpu.make_async_remote_copy(
            st.at[1 - side, :, span(i)], r1.at[:, span(i)], s1_send.at[i], s1_recv.at[i],
            device_id=(partner, head), device_id_type=MESH,
        )
        for i in range(CHUNKS)
    ]
    for copy in first_copies:
        copy.start()

    scaled_2, grads_2 = split(scaled), split(grads)
    inner = dot3(read, write_t, 1, 0)
    lane = lax.broadcasted_iota(jnp.int32, (tokens, channels), 1) // width
    rel_cols = jnp.concatenate([rel] * (8 // heads), axis=0).T
    lower = row_ids >= col_ids

    def near(h):
        gap = rel_cols[:, h : h + 1] - rel[h : h + 1, :]
        decay = jnp.where(lower, jnp.exp(jnp.where(lower, gap, 0.0)), 0.0)
        mixed = split(inner * decay)
        mine = lane == h

        def only(pair):
            return tuple(jnp.where(mine, part.astype(F32), 0.0).astype(BF16) for part in pair)

        scaled_h, grads_h = only(scaled_2), only(grads_2)
        out_h = dot3(mixed, scaled_h, 1, 0)
        back_h = dot3(mixed, grads_h, 0, 0)
        pair_h = decay * dot3(grads_2, scaled_h, 1, 1)
        if h == 0:
            out_ref[...] = out_h
            back[...] = back_h
            wsum[...] = pair_h
        else:
            out_ref[...] += out_h
            back[...] += back_h
            wsum[...] += pair_h

    is_first = side == 0

    def rows_of(i):
        return slice(PAD + i * piece, PAD + (i + 1) * piece)

    def pair_parts(i):
        own, other = st[side, :, rows_of(i)], r1[:, rows_of(i)]
        own_decay, other_decay = st[side, 0, :PAD], r1[0, :PAD]
        return (
            jnp.where(is_first, own, other),
            jnp.where(is_first, other, own),
            spread(jnp.where(is_first, own_decay, other_decay)),
            spread(jnp.where(is_first, other_decay, own_decay)),
        )

    z_copies = []

    def send_totals(i):
        first_copies[i].wait()
        part_0, part_1, decay_0, decay_1 = pair_parts(i)
        tz[0, rows_of(i)] = decay_1 * part_0[0] + part_1[0]
        tz[1, rows_of(i)] = part_0[1] + decay_0 * part_1[1]
        if i == 0:
            for d in range(2):
                tz[d, :PAD] = decay_0[:PAD] * decay_1[:PAD]
        for k in range(1, m):
            peer_row = lax.rem(row + k, m)
            direction = jnp.where(peer_row > row, 0, 1)
            copy = pltpu.make_async_remote_copy(
                tz.at[direction, span(i)], zbuf.at[row, span(i)],
                z_send.at[i, k - 1], z_recv.at[i, row],
                device_id=(peer_row * 2 + side, head), device_id_type=MESH,
            )
            copy.start()
            z_copies.append(copy)

    last_copies = []

    def send_entering(i):
        def joined(j, carried):
            pltpu.make_async_remote_copy(
                tz.at[0, span(i)], zbuf.at[j, span(i)], z_send.at[i, 0], z_recv.at[i, j],
                device_id=(partner, head), device_id_type=MESH,
            ).wait_recv()
            return zbuf[j, rows_of(i)] + spread(zbuf[j, :PAD]) * carried

        zero = jnp.zeros((piece, half), F32)
        carry_f = lax.fori_loop(0, row, joined, zero)
        carry_b = lax.fori_loop(0, m - 1 - row, lambda k, c: joined(m - 1 - k, c), zero)
        part_0, part_1, decay_0, decay_1 = pair_parts(i)
        enter_f = (carry_f, decay_0 * carry_f + part_0[0])
        enter_b = (part_1[1] + decay_1 * carry_b, carry_b)
        for d, pair in enumerate((enter_f, enter_b)):
            fs[side, d, i * piece : (i + 1) * piece] = jnp.where(is_first, pair[0], pair[1])
            fsend[d, i * piece : (i + 1) * piece] = jnp.where(is_first, pair[1], pair[0])
        here = pl.ds(i * piece, piece)
        copy = pltpu.make_async_remote_copy(
            fsend.at[:, here], fs.at[side, :, here], s3_send.at[i], s3_recv.at[i],
            device_id=(partner, head), device_id_type=MESH,
        )
        copy.start()
        last_copies.append(copy)

    near(0)
    send_totals(0)
    near(1)
    for i in range(1, CHUNKS):
        send_totals(i)
    near(2)
    send_entering(0)
    near(3)
    mixed_sums = split(wsum[...])
    read_near = dot3(mixed_sums, write, 1, 0)
    write_near = dot3(mixed_sums, read, 0, 0)
    for i in range(1, CHUNKS):
        send_entering(i)
    for copy in last_copies:
        copy.wait()

    state_f = split(jnp.concatenate([fs[0, 0], fs[1, 0]], axis=1))
    state_b = split(jnp.concatenate([fs[0, 1], fs[1, 1]], axis=1))
    write_all = write_near + dot3(outof_s, state_b, 1, 1)
    read_all = read_near + dot3(into_g, state_f, 1, 1)
    for j in range(nh):
        tot[j, :ck] = write_all[j * ck : (j + 1) * ck]
        tot[j, ck:] = read_all[j * ck : (j + 1) * ck]
    h_copies = []
    for k in range(1, nh):
        peer = lax.rem(head + k, nh)
        copy = pltpu.make_async_remote_copy(
            tot.at[peer], rs.at[k - 1], h_send.at[k - 1], h_recv.at[k - 1],
            device_id=(ctx, peer), device_id_type=MESH,
        )
        copy.start()
        h_copies.append(copy)

    out_ref[...] += into_w * dot3(read, state_f, 1, 0)
    stores[0].start()
    back_all = back[...] + outof_w * dot3(write, state_b, 1, 0)
    gin_ref[...] = step_w * back_all
    stores[1].start()
    pick_row = lax.broadcasted_iota(jnp.int32, (16, channels), 0)
    pick_col = lax.broadcasted_iota(jnp.int32, (16, channels), 1) // width
    pick = jnp.where(pick_row == pick_col, 1.0, 0.0).astype(BF16)
    high, low = split(x_ref[...] * back_all)
    nt = (((1,), (1,)), ((), ()))
    steps = lax.dot_general(pick, high, nt, preferred_element_type=F32) + lax.dot_general(
        pick, low, nt, preferred_element_type=F32
    )
    gstep_ref[...] = steps[:heads]
    stores[2].start()

    result = tot[head]
    for k, copy in enumerate(h_copies):
        copy.wait()
        result = result + rs[k]
    wg_ref[...] = result[:ck]
    stores[3].start()
    rg_ref[...] = result[ck:]
    stores[4].start()
    for copy in z_copies:
        copy.wait_send()
    for store in stores:
        store.wait()


def place(*refs):
    count = len(refs) // 2
    sems = refs[-1]
    copies = [
        pltpu.make_async_copy(refs[i], refs[count + i], sems.at[i]) for i in range(count)
    ]
    for copy in copies:
        copy.start()
    for copy in copies:
        copy.wait()


def solution(mesh):
    n, nh = mesh.shape["ctx"], mesh.shape["head"]
    m = n // 2

    def shards(head_input, step_size, log_decay, write_proj, read_proj, grad_out):
        tokens, channels = head_input.shape
        heads = step_size.shape[0]
        state = write_proj.shape[1]
        half, ck = channels // 2, tokens // nh
        hbm = pl.BlockSpec(memory_space=pltpu.HBM)
        dma = pltpu.SemaphoreType.DMA
        shapes = (
            jax.ShapeDtypeStruct((tokens, channels), F32),
            jax.ShapeDtypeStruct((tokens, channels), F32),
            jax.ShapeDtypeStruct((heads, tokens), F32),
            jax.ShapeDtypeStruct((ck, state), F32),
            jax.ShapeDtypeStruct((ck, state), F32),
        )
        results = pl.pallas_call(
            functools.partial(kernel, n, nh),
            out_shape=shapes,
            in_specs=[hbm] * 6,
            out_specs=(hbm,) * 5,
            scratch_shapes=[
                pltpu.VMEM((tokens, channels), F32),
                pltpu.VMEM((heads, tokens), F32),
                pltpu.VMEM((heads, tokens), F32),
                pltpu.VMEM((tokens, state), F32),
                pltpu.VMEM((tokens, state), F32),
                pltpu.VMEM((tokens, channels), F32),
                *(pltpu.VMEM(shape.shape, F32) for shape in shapes),
                pltpu.VMEM((2, 2, state + PAD, half), F32),
                pltpu.VMEM((2, state + PAD, half), F32),
                pltpu.VMEM((2, state + PAD, half), F32),
                pltpu.VMEM((m, state + PAD, half), F32),
                pltpu.VMEM((2, state, half), F32),
                pltpu.VMEM((2, 2, state, half), F32),
                pltpu.VMEM((nh, 2 * ck, state), F32),
                pltpu.VMEM((nh - 1, 2 * ck, state), F32),
                pltpu.VMEM((tokens, tokens), F32),
                pltpu.VMEM((tokens, channels), F32),
                dma((6,)), dma((5,)),
                dma((CHUNKS,)), dma((CHUNKS,)),
                dma((CHUNKS, m - 1)), dma((CHUNKS, m)),
                dma((CHUNKS,)), dma((CHUNKS,)),
                dma((nh - 1,)), dma((nh - 1,)),
            ],
            compiler_params=pltpu.CompilerParams(
                collective_id=0, has_side_effects=True, vmem_limit_bytes=GRANT
            ),
        )(head_input, step_size, log_decay, write_proj, read_proj, grad_out)
        return pl.pallas_call(
            place,
            out_shape=shapes,
            in_specs=[hbm] * 5,
            out_specs=(hbm,) * 5,
            scratch_shapes=[dma((5,))],
            compiler_params=pltpu.CompilerParams(vmem_limit_bytes=GRANT),
        )(*results)

    return jax.shard_map(
        shards,
        mesh=mesh,
        in_specs=(
            P("ctx", "head"), P("head", "ctx"), P("head", "ctx"),
            P("ctx", None), P("ctx", None), P("ctx", "head"),
        ),
        out_specs=(
            P("ctx", "head"), P("ctx", "head"), P("head", "ctx"),
            P(("ctx", "head"), None), P(("ctx", "head"), None),
        ),
        check_vma=False,
    )
```

```python
import functools

import jax
import jax.numpy as jnp
from jax import lax
from jax.experimental import pallas as pl
from jax.experimental.pallas import tpu as pltpu
from jax.sharding import PartitionSpec as P

MESH = pl.DeviceIdType.MESH
F32 = jnp.float32
BF16 = jnp.bfloat16
PAD = 8
GRANT = 60 * 2**20
CHUNKS = 2


def split(x):
    high = x.astype(BF16)
    return high, (x - high.astype(F32)).astype(BF16)


def dot3(a, b, ca, cb):
    dims = (((ca,), (cb,)), ((), ()))
    dot = functools.partial(lax.dot_general, dimension_numbers=dims, preferred_element_type=F32)
    return dot(a[0], b[0]) + (dot(a[0], b[1]) + dot(a[1], b[0]))


def thirds(rows):
    zeros = jnp.zeros((16 - rows.shape[0], rows.shape[1]), F32)
    pieces = []
    for _ in range(3):
        piece = rows.astype(BF16)
        rows = rows - piece.astype(F32)
        pieces.append(jnp.concatenate([piece.astype(F32), zeros], axis=0))
    return jnp.concatenate(pieces, axis=0).astype(BF16)


def kernel(
    n, nh,
    x_hbm, step_hbm, log_hbm, b_hbm, c_hbm, g_hbm,
    out_hbm, gin_hbm, gstep_hbm, wg_hbm, rg_hbm,
    x_ref, step_ref, log_ref, b_ref, c_ref, g_ref,
    out_ref, gin_ref, gstep_ref, wg_ref, rg_ref,
    st, r1, tz, zbuf, fsend, fs, tot, rs, wsum, back,
    in_sem, out_sem, s1_send, s1_recv, z_send, z_recv, s3_send, s3_recv, h_send, h_recv,
):
    tokens, channels = x_ref.shape
    heads = step_ref.shape[0]
    width = channels // heads
    state = b_ref.shape[1]
    half = channels // 2
    m = n // 2
    ck = tokens // nh
    piece = state // CHUNKS

    ctx, head = lax.axis_index("ctx"), lax.axis_index("head")
    side, row = lax.rem(ctx, 2), lax.div(ctx, 2)
    partner = row * 2 + (1 - side)

    barrier = pltpu.get_barrier_semaphore()
    pl.semaphore_signal(barrier, inc=1, device_id=(partner, head), device_id_type=MESH)
    for k in range(1, m):
        peer = lax.rem(row + k, m) * 2 + side
        pl.semaphore_signal(barrier, inc=1, device_id=(peer, head), device_id_type=MESH)
    for k in range(1, nh):
        pl.semaphore_signal(
            barrier, inc=1, device_id=(ctx, lax.rem(head + k, nh)), device_id_type=MESH
        )

    loads = [
        pltpu.make_async_copy(source, target, in_sem.at[i])
        for i, (source, target) in enumerate((
            (log_hbm, log_ref), (step_hbm, step_ref), (b_hbm, b_ref),
            (c_hbm, c_ref), (x_hbm, x_ref), (g_hbm, g_ref),
        ))
    ]
    for load in loads:
        load.start()

    stores = [
        pltpu.make_async_copy(source, target, out_sem.at[i])
        for i, (source, target) in enumerate((
            (out_ref, out_hbm), (gin_ref, gin_hbm), (gstep_ref, gstep_hbm),
            (wg_ref, wg_hbm), (rg_ref, rg_hbm),
        ))
    ]

    mid = tokens // 2
    row_ids = lax.broadcasted_iota(jnp.int32, (tokens, tokens), 0)
    col_ids = lax.broadcasted_iota(jnp.int32, (tokens, tokens), 1)
    weights = jnp.where(
        (row_ids <= col_ids) & (row_ids >= mid),
        1.0,
        jnp.where((row_ids > col_ids) & (row_ids < mid), -1.0, 0.0),
    ).astype(BF16)
    pick_row = lax.broadcasted_iota(jnp.int32, (48, 3 * channels), 0) % 16
    pick_col = lax.broadcasted_iota(jnp.int32, (48, 3 * channels), 1) // width
    expand = jnp.where(pick_row == pick_col, 1.0, 0.0).astype(BF16)

    loads[0].wait()
    logs = log_ref[...]
    sums = jnp.dot(thirds(logs), weights, preferred_element_type=F32)
    rel = sums[:heads] + sums[16 : 16 + heads] + sums[32 : 32 + heads]
    before = jnp.sum(logs[:, :mid], axis=1, keepdims=True)
    last = rel[:, tokens - 1 : tokens]
    into = jnp.exp(rel + before)
    outof = jnp.exp(last - rel)
    loads[1].wait()
    factors = thirds(jnp.concatenate([step_ref[...], into, outof], axis=0))
    wide = lax.dot_general(
        factors, expand, (((0,), (0,)), ((), ())), preferred_element_type=F32
    )
    step_w = wide[:, :channels]
    into_w = wide[:, channels : 2 * channels]
    outof_w = wide[:, 2 * channels :]

    loads[2].wait()
    write, write_t = split(b_ref[...]), split(b_ref[...].T)
    loads[3].wait()
    read, read_t = split(c_ref[...]), split(c_ref[...].T)
    loads[4].wait()
    scaled = x_ref[...] * step_w
    outof_s = split(outof_w * scaled)
    fwd = dot3(write_t, outof_s, 1, 0)
    loads[5].wait()
    grads = g_ref[...]
    into_g = split(into_w * grads)
    bwd = dot3(read_t, into_g, 1, 0)
    decay_rows = jnp.broadcast_to(into_w[tokens - 1 : tokens], (PAD, channels))
    for j in range(2):
        for d, whole in enumerate((fwd, bwd)):
            st[j, d, :PAD] = decay_rows[:, j * half : (j + 1) * half]
            st[j, d, PAD:] = whole[:, j * half : (j + 1) * half]

    def span(i):
        return pl.ds(0, PAD + piece) if i == 0 else pl.ds(PAD + i * piece, piece)

    def spread(decay):
        return jnp.concatenate([decay] * (piece // PAD), axis=0)

    pl.semaphore_wait(barrier, 1 + (m - 1) + (nh - 1))
    first_copies = [
        pltpu.make_async_remote_copy(
            st.at[1 - side, :, span(i)], r1.at[:, span(i)], s1_send.at[i], s1_recv.at[i],
            device_id=(partner, head), device_id_type=MESH,
        )
        for i in range(CHUNKS)
    ]
    for copy in first_copies:
        copy.start()

    scaled_2, grads_2 = split(scaled), split(grads)
    inner = dot3(read, write_t, 1, 0)
    lane = lax.broadcasted_iota(jnp.int32, (tokens, channels), 1) // width
    rel_cols = jnp.concatenate([rel] * (8 // heads), axis=0).T
    lower = row_ids >= col_ids

    def near(h):
        gap = rel_cols[:, h : h + 1] - rel[h : h + 1, :]
        decay = jnp.where(lower, jnp.exp(jnp.where(lower, gap, 0.0)), 0.0)
        mixed = split(inner * decay)
        mine = lane == h

        def only(pair):
            return tuple(jnp.where(mine, part.astype(F32), 0.0).astype(BF16) for part in pair)

        scaled_h, grads_h = only(scaled_2), only(grads_2)
        out_h = dot3(mixed, scaled_h, 1, 0)
        back_h = dot3(mixed, grads_h, 0, 0)
        pair_h = decay * dot3(grads_2, scaled_h, 1, 1)
        if h == 0:
            out_ref[...] = out_h
            back[...] = back_h
            wsum[...] = pair_h
        else:
            out_ref[...] += out_h
            back[...] += back_h
            wsum[...] += pair_h

    is_first = side == 0

    def rows_of(i):
        return slice(PAD + i * piece, PAD + (i + 1) * piece)

    def pair_parts(i):
        own, other = st[side, :, rows_of(i)], r1[:, rows_of(i)]
        own_decay, other_decay = st[side, 0, :PAD], r1[0, :PAD]
        return (
            jnp.where(is_first, own, other),
            jnp.where(is_first, other, own),
            spread(jnp.where(is_first, own_decay, other_decay)),
            spread(jnp.where(is_first, other_decay, own_decay)),
        )

    z_copies = []

    def send_totals(i):
        first_copies[i].wait()
        part_0, part_1, decay_0, decay_1 = pair_parts(i)
        tz[0, rows_of(i)] = decay_1 * part_0[0] + part_1[0]
        tz[1, rows_of(i)] = part_0[1] + decay_0 * part_1[1]
        if i == 0:
            for d in range(2):
                tz[d, :PAD] = decay_0[:PAD] * decay_1[:PAD]
        for k in range(1, m):
            peer_row = lax.rem(row + k, m)
            direction = jnp.where(peer_row > row, 0, 1)
            copy = pltpu.make_async_remote_copy(
                tz.at[direction, span(i)], zbuf.at[row, span(i)],
                z_send.at[i, k - 1], z_recv.at[i, row],
                device_id=(peer_row * 2 + side, head), device_id_type=MESH,
            )
            copy.start()
            z_copies.append(copy)

    last_copies = []

    def send_entering(i):
        def joined(j, carried):
            pltpu.make_async_remote_copy(
                tz.at[0, span(i)], zbuf.at[j, span(i)], z_send.at[i, 0], z_recv.at[i, j],
                device_id=(partner, head), device_id_type=MESH,
            ).wait_recv()
            return zbuf[j, rows_of(i)] + spread(zbuf[j, :PAD]) * carried

        zero = jnp.zeros((piece, half), F32)
        carry_f = lax.fori_loop(0, row, joined, zero)
        carry_b = lax.fori_loop(0, m - 1 - row, lambda k, c: joined(m - 1 - k, c), zero)
        part_0, part_1, decay_0, decay_1 = pair_parts(i)
        enter_f = (carry_f, decay_0 * carry_f + part_0[0])
        enter_b = (part_1[1] + decay_1 * carry_b, carry_b)
        for d, pair in enumerate((enter_f, enter_b)):
            fs[side, d, i * piece : (i + 1) * piece] = jnp.where(is_first, pair[0], pair[1])
            fsend[d, i * piece : (i + 1) * piece] = jnp.where(is_first, pair[1], pair[0])
        here = pl.ds(i * piece, piece)
        copy = pltpu.make_async_remote_copy(
            fsend.at[:, here], fs.at[side, :, here], s3_send.at[i], s3_recv.at[i],
            device_id=(partner, head), device_id_type=MESH,
        )
        copy.start()
        last_copies.append(copy)

    near(0)
    send_totals(0)
    near(1)
    for i in range(1, CHUNKS):
        send_totals(i)
    near(2)
    send_entering(0)
    near(3)
    mixed_sums = split(wsum[...])
    read_near = dot3(mixed_sums, write, 1, 0)
    write_near = dot3(mixed_sums, read, 0, 0)
    for i in range(1, CHUNKS):
        send_entering(i)
    for copy in last_copies:
        copy.wait()

    state_f = split(jnp.concatenate([fs[0, 0], fs[1, 0]], axis=1))
    state_b = split(jnp.concatenate([fs[0, 1], fs[1, 1]], axis=1))
    write_all = write_near + dot3(outof_s, state_b, 1, 1)
    read_all = read_near + dot3(into_g, state_f, 1, 1)
    for j in range(nh):
        tot[j, :ck] = write_all[j * ck : (j + 1) * ck]
        tot[j, ck:] = read_all[j * ck : (j + 1) * ck]
    h_copies = []
    for k in range(1, nh):
        peer = lax.rem(head + k, nh)
        copy = pltpu.make_async_remote_copy(
            tot.at[peer], rs.at[k - 1], h_send.at[k - 1], h_recv.at[k - 1],
            device_id=(ctx, peer), device_id_type=MESH,
        )
        copy.start()
        h_copies.append(copy)

    out_ref[...] += into_w * dot3(read, state_f, 1, 0)
    stores[0].start()
    back_all = back[...] + outof_w * dot3(write, state_b, 1, 0)
    gin_ref[...] = step_w * back_all
    stores[1].start()
    pick_row = lax.broadcasted_iota(jnp.int32, (16, channels), 0)
    pick_col = lax.broadcasted_iota(jnp.int32, (16, channels), 1) // width
    pick = jnp.where(pick_row == pick_col, 1.0, 0.0).astype(BF16)
    high, low = split(x_ref[...] * back_all)
    nt = (((1,), (1,)), ((), ()))
    steps = lax.dot_general(pick, high, nt, preferred_element_type=F32) + lax.dot_general(
        pick, low, nt, preferred_element_type=F32
    )
    gstep_ref[...] = steps[:heads]
    stores[2].start()

    result = tot[head]
    for k, copy in enumerate(h_copies):
        copy.wait()
        result = result + rs[k]
    wg_ref[...] = result[:ck]
    stores[3].start()
    rg_ref[...] = result[ck:]
    stores[4].start()
    for copy in z_copies:
        copy.wait_send()
    for store in stores:
        store.wait()


def place(*refs):
    count = (len(refs) - 2) // 3
    sources, targets, held = refs[:count], refs[count : 2 * count], refs[2 * count : 3 * count]
    in_sem, out_sem = refs[-2:]
    loads = [pltpu.make_async_copy(sources[i], held[i], in_sem.at[i]) for i in range(count)]
    stores = [pltpu.make_async_copy(held[i], targets[i], out_sem.at[i]) for i in range(count)]
    for load in loads:
        load.start()
    for load, store in zip(loads, stores):
        load.wait()
        store.start()
    for store in stores:
        store.wait()


def solution(mesh):
    n, nh = mesh.shape["ctx"], mesh.shape["head"]
    m = n // 2

    def shards(head_input, step_size, log_decay, write_proj, read_proj, grad_out):
        tokens, channels = head_input.shape
        heads = step_size.shape[0]
        state = write_proj.shape[1]
        half, ck = channels // 2, tokens // nh
        hbm = pl.BlockSpec(memory_space=pltpu.HBM)
        dma = pltpu.SemaphoreType.DMA
        shapes = (
            jax.ShapeDtypeStruct((tokens, channels), F32),
            jax.ShapeDtypeStruct((tokens, channels), F32),
            jax.ShapeDtypeStruct((heads, tokens), F32),
            jax.ShapeDtypeStruct((ck, state), F32),
            jax.ShapeDtypeStruct((ck, state), F32),
        )
        results = pl.pallas_call(
            functools.partial(kernel, n, nh),
            out_shape=shapes,
            in_specs=[hbm] * 6,
            out_specs=(hbm,) * 5,
            scratch_shapes=[
                pltpu.VMEM((tokens, channels), F32),
                pltpu.VMEM((heads, tokens), F32),
                pltpu.VMEM((heads, tokens), F32),
                pltpu.VMEM((tokens, state), F32),
                pltpu.VMEM((tokens, state), F32),
                pltpu.VMEM((tokens, channels), F32),
                *(pltpu.VMEM(shape.shape, F32) for shape in shapes),
                pltpu.VMEM((2, 2, state + PAD, half), F32),
                pltpu.VMEM((2, state + PAD, half), F32),
                pltpu.VMEM((2, state + PAD, half), F32),
                pltpu.VMEM((m, state + PAD, half), F32),
                pltpu.VMEM((2, state, half), F32),
                pltpu.VMEM((2, 2, state, half), F32),
                pltpu.VMEM((nh, 2 * ck, state), F32),
                pltpu.VMEM((nh - 1, 2 * ck, state), F32),
                pltpu.VMEM((tokens, tokens), F32),
                pltpu.VMEM((tokens, channels), F32),
                dma((6,)), dma((5,)),
                dma((CHUNKS,)), dma((CHUNKS,)),
                dma((CHUNKS, m - 1)), dma((CHUNKS, m)),
                dma((CHUNKS,)), dma((CHUNKS,)),
                dma((nh - 1,)), dma((nh - 1,)),
            ],
            compiler_params=pltpu.CompilerParams(
                collective_id=0, has_side_effects=True, vmem_limit_bytes=GRANT
            ),
        )(head_input, step_size, log_decay, write_proj, read_proj, grad_out)
        return pl.pallas_call(
            place,
            out_shape=shapes,
            in_specs=[hbm] * 5,
            out_specs=(hbm,) * 5,
            scratch_shapes=[
                *(pltpu.VMEM(shape.shape, F32) for shape in shapes), dma((5,)), dma((5,)),
            ],
            compiler_params=pltpu.CompilerParams(vmem_limit_bytes=GRANT),
        )(*results)

    return jax.shard_map(
        shards,
        mesh=mesh,
        in_specs=(
            P("ctx", "head"), P("head", "ctx"), P("head", "ctx"),
            P("ctx", None), P("ctx", None), P("ctx", "head"),
        ),
        out_specs=(
            P("ctx", "head"), P("ctx", "head"), P("head", "ctx"),
            P(("ctx", "head"), None), P(("ctx", "head"), None),
        ),
        check_vma=False,
    )
```

```python
import functools

import jax
import jax.numpy as jnp
from jax import lax
from jax.experimental import pallas as pl
from jax.experimental.pallas import tpu as pltpu
from jax.sharding import PartitionSpec as P

MESH = pl.DeviceIdType.MESH
F32 = jnp.float32
BF16 = jnp.bfloat16
PAD = 8
GRANT = 60 * 2**20
CHUNKS = 4


def split(x):
    high = x.astype(BF16)
    return high, (x - high.astype(F32)).astype(BF16)


def dot3(a, b, ca, cb):
    left = jnp.concatenate([a[0], a[0], a[1]], axis=ca)
    right = jnp.concatenate([b[0], b[1], b[0]], axis=cb)
    return lax.dot_general(left, right, (((ca,), (cb,)), ((), ())), preferred_element_type=F32)


def thirds(rows):
    zeros = jnp.zeros((16 - rows.shape[0], rows.shape[1]), F32)
    pieces = []
    for _ in range(3):
        piece = rows.astype(BF16)
        rows = rows - piece.astype(F32)
        pieces.append(jnp.concatenate([piece.astype(F32), zeros], axis=0))
    return jnp.concatenate(pieces, axis=0).astype(BF16)


def kernel(
    n, nh,
    x_hbm, step_hbm, log_hbm, b_hbm, c_hbm, g_hbm,
    out_hbm, gin_hbm, gstep_hbm, wg_hbm, rg_hbm,
    x_ref, step_ref, log_ref, b_ref, c_ref, g_ref,
    out_ref, gin_ref, gstep_ref, wg_ref, rg_ref,
    st, r1, tz, zbuf, fsend, fs, tot, rs, wsum, back,
    in_sem, out_sem, s1_send, s1_recv, z_send, z_recv, s3_send, s3_recv, h_send, h_recv,
):
    tokens, channels = x_ref.shape
    heads = step_ref.shape[0]
    width = channels // heads
    state = b_ref.shape[1]
    half = channels // 2
    m = n // 2
    ck = tokens // nh
    piece = state // CHUNKS

    ctx, head = lax.axis_index("ctx"), lax.axis_index("head")
    side, row = lax.rem(ctx, 2), lax.div(ctx, 2)
    partner = row * 2 + (1 - side)

    barrier = pltpu.get_barrier_semaphore()
    pl.semaphore_signal(barrier, inc=1, device_id=(partner, head), device_id_type=MESH)
    for k in range(1, m):
        peer = lax.rem(row + k, m) * 2 + side
        pl.semaphore_signal(barrier, inc=1, device_id=(peer, head), device_id_type=MESH)
    for k in range(1, nh):
        pl.semaphore_signal(
            barrier, inc=1, device_id=(ctx, lax.rem(head + k, nh)), device_id_type=MESH
        )

    loads = [
        pltpu.make_async_copy(source, target, in_sem.at[i])
        for i, (source, target) in enumerate((
            (log_hbm, log_ref), (step_hbm, step_ref), (b_hbm, b_ref),
            (c_hbm, c_ref), (x_hbm, x_ref), (g_hbm, g_ref),
        ))
    ]
    for load in loads:
        load.start()

    stores = [
        pltpu.make_async_copy(source, target, out_sem.at[i])
        for i, (source, target) in enumerate((
            (out_ref, out_hbm), (gin_ref, gin_hbm), (gstep_ref, gstep_hbm),
            (wg_ref, wg_hbm), (rg_ref, rg_hbm),
        ))
    ]

    mid = tokens // 2
    row_ids = lax.broadcasted_iota(jnp.int32, (tokens, tokens), 0)
    col_ids = lax.broadcasted_iota(jnp.int32, (tokens, tokens), 1)
    weights = jnp.where(
        (row_ids <= col_ids) & (row_ids >= mid),
        1.0,
        jnp.where((row_ids > col_ids) & (row_ids < mid), -1.0, 0.0),
    ).astype(BF16)
    pick_row = lax.broadcasted_iota(jnp.int32, (48, 3 * channels), 0) % 16
    pick_col = lax.broadcasted_iota(jnp.int32, (48, 3 * channels), 1) // width
    expand = jnp.where(pick_row == pick_col, 1.0, 0.0).astype(BF16)

    loads[0].wait()
    logs = log_ref[...]
    sums = jnp.dot(thirds(logs), weights, preferred_element_type=F32)
    rel = sums[:heads] + sums[16 : 16 + heads] + sums[32 : 32 + heads]
    before = jnp.sum(logs[:, :mid], axis=1, keepdims=True)
    last = rel[:, tokens - 1 : tokens]
    into = jnp.exp(rel + before)
    outof = jnp.exp(last - rel)
    loads[1].wait()
    factors = thirds(jnp.concatenate([step_ref[...], into, outof], axis=0))
    wide = lax.dot_general(
        factors, expand, (((0,), (0,)), ((), ())), preferred_element_type=F32
    )
    step_w = wide[:, :channels]
    into_w = wide[:, channels : 2 * channels]
    outof_w = wide[:, 2 * channels :]

    loads[2].wait()
    write, write_t = split(b_ref[...]), split(b_ref[...].T)
    loads[3].wait()
    read, read_t = split(c_ref[...]), split(c_ref[...].T)
    loads[4].wait()
    scaled = x_ref[...] * step_w
    outof_s = split(outof_w * scaled)
    fwd = dot3(write_t, outof_s, 1, 0)
    loads[5].wait()
    grads = g_ref[...]
    into_g = split(into_w * grads)
    bwd = dot3(read_t, into_g, 1, 0)
    decay_rows = jnp.broadcast_to(into_w[tokens - 1 : tokens], (PAD, channels))
    for j in range(2):
        for d, whole in enumerate((fwd, bwd)):
            st[j, d, :PAD] = decay_rows[:, j * half : (j + 1) * half]
            st[j, d, PAD:] = whole[:, j * half : (j + 1) * half]

    def span(i):
        return pl.ds(0, PAD + piece) if i == 0 else pl.ds(PAD + i * piece, piece)

    def spread(decay):
        return jnp.concatenate([decay] * (piece // PAD), axis=0)

    pl.semaphore_wait(barrier, 1 + (m - 1) + (nh - 1))
    first_copies = [
        pltpu.make_async_remote_copy(
            st.at[1 - side, :, span(i)], r1.at[:, span(i)], s1_send.at[i], s1_recv.at[i],
            device_id=(partner, head), device_id_type=MESH,
        )
        for i in range(CHUNKS)
    ]
    for copy in first_copies:
        copy.start()

    scaled_2, grads_2 = split(scaled), split(grads)
    panels = ((0, mid), (mid, tokens))

    def part(pair, rows, columns=slice(None)):
        return tuple(x[rows, columns] for x in pair)

    inner = [
        dot3(part(read, slice(lo, hi)), part(write_t, slice(None), slice(0, hi)), 1, 0)
        for lo, hi in panels
    ]
    lanes = 2 * width
    lane = lax.broadcasted_iota(jnp.int32, (1, lanes), 1) // width
    rel_cols = jnp.concatenate([rel] * (8 // heads), axis=0).T
    out_ref[...] = jnp.zeros_like(out_ref)
    back[...] = jnp.zeros_like(back)
    wsum[...] = jnp.zeros_like(wsum)

    def near(h):
        here = slice(h // 2 * lanes, (h // 2 + 1) * lanes)
        mask = jnp.where(lane == h % 2, 1.0, 0.0).astype(BF16)
        scaled_h = tuple(x[:, here] * mask for x in scaled_2)
        grads_h = tuple(x[:, here] * mask for x in grads_2)
        for k, (lo, hi) in enumerate(panels):
            rows, reach = slice(lo, hi), slice(0, hi)
            gap = rel_cols[rows, h : h + 1] - rel[h : h + 1, reach]
            lower = row_ids[rows, reach] >= col_ids[rows, reach]
            decay = jnp.exp(jnp.where(lower, gap, -1e30))
            mixed = split(inner[k] * decay)
            out_ref[rows, here] += dot3(mixed, part(scaled_h, reach), 1, 0)
            back[reach, here] += dot3(mixed, part(grads_h, rows), 0, 0)
            wsum[rows, reach] += decay * dot3(
                part(grads_2, rows, here), part(scaled_h, reach), 1, 1
            )

    is_first = side == 0

    def rows_of(i):
        return slice(PAD + i * piece, PAD + (i + 1) * piece)

    def pair_parts(i):
        own, other = st[side, :, rows_of(i)], r1[:, rows_of(i)]
        own_decay, other_decay = st[side, 0, :PAD], r1[0, :PAD]
        return (
            jnp.where(is_first, own, other),
            jnp.where(is_first, other, own),
            spread(jnp.where(is_first, own_decay, other_decay)),
            spread(jnp.where(is_first, other_decay, own_decay)),
        )

    z_copies = []

    def send_totals(i):
        first_copies[i].wait()
        part_0, part_1, decay_0, decay_1 = pair_parts(i)
        tz[0, rows_of(i)] = decay_1 * part_0[0] + part_1[0]
        tz[1, rows_of(i)] = part_0[1] + decay_0 * part_1[1]
        if i == 0:
            for d in range(2):
                tz[d, :PAD] = decay_0[:PAD] * decay_1[:PAD]
        for k in range(1, m):
            peer_row = lax.rem(row + k, m)
            direction = jnp.where(peer_row > row, 0, 1)
            copy = pltpu.make_async_remote_copy(
                tz.at[direction, span(i)], zbuf.at[row, span(i)],
                z_send.at[i, k - 1], z_recv.at[i, row],
                device_id=(peer_row * 2 + side, head), device_id_type=MESH,
            )
            copy.start()
            z_copies.append(copy)

    last_copies = []

    def send_entering(i):
        def joined(j, carried):
            pltpu.make_async_remote_copy(
                tz.at[0, span(i)], zbuf.at[j, span(i)], z_send.at[i, 0], z_recv.at[i, j],
                device_id=(partner, head), device_id_type=MESH,
            ).wait_recv()
            return zbuf[j, rows_of(i)] + spread(zbuf[j, :PAD]) * carried

        zero = jnp.zeros((piece, half), F32)
        carry_f = lax.fori_loop(0, row, joined, zero)
        carry_b = lax.fori_loop(0, m - 1 - row, lambda k, c: joined(m - 1 - k, c), zero)
        part_0, part_1, decay_0, decay_1 = pair_parts(i)
        enter_f = (carry_f, decay_0 * carry_f + part_0[0])
        enter_b = (part_1[1] + decay_1 * carry_b, carry_b)
        for d, pair in enumerate((enter_f, enter_b)):
            fs[side, d, i * piece : (i + 1) * piece] = jnp.where(is_first, pair[0], pair[1])
            fsend[d, i * piece : (i + 1) * piece] = jnp.where(is_first, pair[1], pair[0])
        here = pl.ds(i * piece, piece)
        copy = pltpu.make_async_remote_copy(
            fsend.at[:, here], fs.at[side, :, here], s3_send.at[i], s3_recv.at[i],
            device_id=(partner, head), device_id_type=MESH,
        )
        copy.start()
        last_copies.append(copy)

    near(0)
    send_totals(0)
    near(1)
    send_totals(1)
    send_totals(2)
    near(2)
    send_totals(3)
    near(3)
    send_entering(0)
    mixed_sums = split(wsum[...])
    read_near = dot3(mixed_sums, write, 1, 0)
    write_near = dot3(mixed_sums, read, 0, 0)
    for i in range(1, CHUNKS):
        send_entering(i)
    for copy in last_copies:
        copy.wait()

    state_b = split(jnp.concatenate([fs[0, 1], fs[1, 1]], axis=1))
    state_f = split(jnp.concatenate([fs[0, 0], fs[1, 0]], axis=1))
    h_copies = []
    for which, (nearby, factor, far) in enumerate((
        (write_near, outof_s, state_b), (read_near, into_g, state_f),
    )):
        total = nearby + dot3(factor, far, 1, 1)
        for j in range(nh):
            tot[which, j] = total[j * ck : (j + 1) * ck]
        for k in range(1, nh):
            peer = lax.rem(head + k, nh)
            copy = pltpu.make_async_remote_copy(
                tot.at[which, peer], rs.at[which, k - 1],
                h_send.at[which, k - 1], h_recv.at[which, k - 1],
                device_id=(ctx, peer), device_id_type=MESH,
            )
            copy.start()
            h_copies.append(copy)

    out_ref[...] += into_w * dot3(read, state_f, 1, 0)
    stores[0].start()
    back_all = back[...] + outof_w * dot3(write, state_b, 1, 0)
    gin_ref[...] = step_w * back_all
    stores[1].start()
    pick_row = lax.broadcasted_iota(jnp.int32, (16, channels), 0)
    pick_col = lax.broadcasted_iota(jnp.int32, (16, channels), 1) // width
    pick = jnp.where(pick_row == pick_col, 1.0, 0.0).astype(BF16)
    high, low = split(x_ref[...] * back_all)
    nt = (((1,), (1,)), ((), ()))
    steps = lax.dot_general(pick, high, nt, preferred_element_type=F32) + lax.dot_general(
        pick, low, nt, preferred_element_type=F32
    )
    gstep_ref[...] = steps[:heads]
    stores[2].start()

    for which, (target, store) in enumerate(((wg_ref, stores[3]), (rg_ref, stores[4]))):
        result = tot[which, head]
        for k in range(1, nh):
            h_copies[which * (nh - 1) + k - 1].wait()
            result = result + rs[which, k - 1]
        target[...] = result
        store.start()
    for copy in z_copies:
        copy.wait_send()
    for store in stores:
        store.wait()


def place(*refs):
    count = (len(refs) - 2) // 3
    sources, targets, held = refs[:count], refs[count : 2 * count], refs[2 * count : 3 * count]
    in_sem, out_sem = refs[-2:]
    loads = [pltpu.make_async_copy(sources[i], held[i], in_sem.at[i]) for i in range(count)]
    stores = [pltpu.make_async_copy(held[i], targets[i], out_sem.at[i]) for i in range(count)]
    for load in loads:
        load.start()
    for load, store in zip(loads, stores):
        load.wait()
        store.start()
    for store in stores:
        store.wait()


def solution(mesh):
    n, nh = mesh.shape["ctx"], mesh.shape["head"]
    m = n // 2

    def shards(head_input, step_size, log_decay, write_proj, read_proj, grad_out):
        tokens, channels = head_input.shape
        heads = step_size.shape[0]
        state = write_proj.shape[1]
        half, ck = channels // 2, tokens // nh
        hbm = pl.BlockSpec(memory_space=pltpu.HBM)
        dma = pltpu.SemaphoreType.DMA
        shapes = (
            jax.ShapeDtypeStruct((tokens, channels), F32),
            jax.ShapeDtypeStruct((tokens, channels), F32),
            jax.ShapeDtypeStruct((heads, tokens), F32),
            jax.ShapeDtypeStruct((ck, state), F32),
            jax.ShapeDtypeStruct((ck, state), F32),
        )
        results = pl.pallas_call(
            functools.partial(kernel, n, nh),
            out_shape=shapes,
            in_specs=[hbm] * 6,
            out_specs=(hbm,) * 5,
            scratch_shapes=[
                pltpu.VMEM((tokens, channels), F32),
                pltpu.VMEM((heads, tokens), F32),
                pltpu.VMEM((heads, tokens), F32),
                pltpu.VMEM((tokens, state), F32),
                pltpu.VMEM((tokens, state), F32),
                pltpu.VMEM((tokens, channels), F32),
                *(pltpu.VMEM(shape.shape, F32) for shape in shapes),
                pltpu.VMEM((2, 2, state + PAD, half), F32),
                pltpu.VMEM((2, state + PAD, half), F32),
                pltpu.VMEM((2, state + PAD, half), F32),
                pltpu.VMEM((m, state + PAD, half), F32),
                pltpu.VMEM((2, state, half), F32),
                pltpu.VMEM((2, 2, state, half), F32),
                pltpu.VMEM((2, nh, ck, state), F32),
                pltpu.VMEM((2, nh - 1, ck, state), F32),
                pltpu.VMEM((tokens, tokens), F32),
                pltpu.VMEM((tokens, channels), F32),
                dma((6,)), dma((5,)),
                dma((CHUNKS,)), dma((CHUNKS,)),
                dma((CHUNKS, m - 1)), dma((CHUNKS, m)),
                dma((CHUNKS,)), dma((CHUNKS,)),
                dma((2, nh - 1)), dma((2, nh - 1)),
            ],
            compiler_params=pltpu.CompilerParams(
                collective_id=0, has_side_effects=True, vmem_limit_bytes=GRANT
            ),
        )(head_input, step_size, log_decay, write_proj, read_proj, grad_out)
        return pl.pallas_call(
            place,
            out_shape=shapes,
            in_specs=[hbm] * 5,
            out_specs=(hbm,) * 5,
            scratch_shapes=[
                *(pltpu.VMEM(shape.shape, F32) for shape in shapes), dma((5,)), dma((5,)),
            ],
            compiler_params=pltpu.CompilerParams(vmem_limit_bytes=GRANT),
        )(*results)

    return jax.shard_map(
        shards,
        mesh=mesh,
        in_specs=(
            P("ctx", "head"), P("head", "ctx"), P("head", "ctx"),
            P("ctx", None), P("ctx", None), P("ctx", "head"),
        ),
        out_specs=(
            P("ctx", "head"), P("ctx", "head"), P("head", "ctx"),
            P(("ctx", "head"), None), P(("ctx", "head"), None),
        ),
        check_vma=False,
    )
```

```python
import functools

import jax
import jax.numpy as jnp
from jax import lax
from jax.experimental import pallas as pl
from jax.experimental.pallas import tpu as pltpu
from jax.sharding import PartitionSpec as P

MESH = pl.DeviceIdType.MESH
F32 = jnp.float32
BF16 = jnp.bfloat16
PAD = 8
GRANT = 32 * 2**20
CHUNKS = 4


def split(x):
    high = x.astype(BF16)
    return high, (x - high.astype(F32)).astype(BF16)


def dot3(a, b, ca, cb):
    left = jnp.concatenate([a[0], a[0], a[1]], axis=ca)
    right = jnp.concatenate([b[0], b[1], b[0]], axis=cb)
    return lax.dot_general(left, right, (((ca,), (cb,)), ((), ())), preferred_element_type=F32)


def thirds(rows):
    zeros = jnp.zeros((16 - rows.shape[0], rows.shape[1]), F32)
    pieces = []
    for _ in range(3):
        piece = rows.astype(BF16)
        rows = rows - piece.astype(F32)
        pieces.append(jnp.concatenate([piece.astype(F32), zeros], axis=0))
    return jnp.concatenate(pieces, axis=0).astype(BF16)


def kernel(
    n, nh,
    x_hbm, step_hbm, log_hbm, b_hbm, c_hbm, g_hbm,
    out_ref, gin_ref, gstep_ref, wg_ref, rg_ref,
    x_ref, step_ref, log_ref, b_ref, c_ref, g_ref,
    st, r1, tz, zbuf, fsend, fs, tot, rs, wsum, back,
    in_sem, s1_send, s1_recv, z_send, z_recv, s3_send, s3_recv, h_send, h_recv,
):
    tokens, channels = x_ref.shape
    heads = step_ref.shape[0]
    width = channels // heads
    state = b_ref.shape[1]
    half = channels // 2
    m = n // 2
    ck = tokens // nh
    piece = state // CHUNKS

    ctx, head = lax.axis_index("ctx"), lax.axis_index("head")
    side, row = lax.rem(ctx, 2), lax.div(ctx, 2)
    partner = row * 2 + (1 - side)

    barrier = pltpu.get_barrier_semaphore()
    pl.semaphore_signal(barrier, inc=1, device_id=(partner, head), device_id_type=MESH)
    for k in range(1, m):
        peer = lax.rem(row + k, m) * 2 + side
        pl.semaphore_signal(barrier, inc=1, device_id=(peer, head), device_id_type=MESH)
    for k in range(1, nh):
        pl.semaphore_signal(
            barrier, inc=1, device_id=(ctx, lax.rem(head + k, nh)), device_id_type=MESH
        )

    loads = [
        pltpu.make_async_copy(source, target, in_sem.at[i])
        for i, (source, target) in enumerate((
            (log_hbm, log_ref), (step_hbm, step_ref), (b_hbm, b_ref),
            (c_hbm, c_ref), (x_hbm, x_ref), (g_hbm, g_ref),
        ))
    ]
    for load in loads:
        load.start()

    mid = tokens // 2
    row_ids = lax.broadcasted_iota(jnp.int32, (tokens, tokens), 0)
    col_ids = lax.broadcasted_iota(jnp.int32, (tokens, tokens), 1)
    weights = jnp.where(
        (row_ids <= col_ids) & (row_ids >= mid),
        1.0,
        jnp.where((row_ids > col_ids) & (row_ids < mid), -1.0, 0.0),
    ).astype(BF16)
    pick_row = lax.broadcasted_iota(jnp.int32, (48, 3 * channels), 0) % 16
    pick_col = lax.broadcasted_iota(jnp.int32, (48, 3 * channels), 1) // width
    expand = jnp.where(pick_row == pick_col, 1.0, 0.0).astype(BF16)

    loads[0].wait()
    logs = log_ref[...]
    sums = jnp.dot(thirds(logs), weights, preferred_element_type=F32)
    rel = sums[:heads] + sums[16 : 16 + heads] + sums[32 : 32 + heads]
    before = jnp.sum(logs[:, :mid], axis=1, keepdims=True)
    last = rel[:, tokens - 1 : tokens]
    into = jnp.exp(rel + before)
    outof = jnp.exp(last - rel)
    loads[1].wait()
    factors = thirds(jnp.concatenate([step_ref[...], into, outof], axis=0))
    wide = lax.dot_general(
        factors, expand, (((0,), (0,)), ((), ())), preferred_element_type=F32
    )
    step_w = wide[:, :channels]
    into_w = wide[:, channels : 2 * channels]
    outof_w = wide[:, 2 * channels :]

    loads[2].wait()
    write, write_t = split(b_ref[...]), split(b_ref[...].T)
    loads[3].wait()
    read, read_t = split(c_ref[...]), split(c_ref[...].T)
    loads[4].wait()
    scaled = x_ref[...] * step_w
    outof_s = split(outof_w * scaled)
    fwd = dot3(write_t, outof_s, 1, 0)
    loads[5].wait()
    grads = g_ref[...]
    into_g = split(into_w * grads)
    bwd = dot3(read_t, into_g, 1, 0)
    decay_rows = jnp.broadcast_to(into_w[tokens - 1 : tokens], (PAD, channels))
    for j in range(2):
        for d, whole in enumerate((fwd, bwd)):
            st[j, d, :PAD] = decay_rows[:, j * half : (j + 1) * half]
            st[j, d, PAD:] = whole[:, j * half : (j + 1) * half]

    def span(i):
        return pl.ds(0, PAD + piece) if i == 0 else pl.ds(PAD + i * piece, piece)

    def spread(decay):
        return jnp.concatenate([decay] * (piece // PAD), axis=0)

    pl.semaphore_wait(barrier, 1 + (m - 1) + (nh - 1))
    first_copies = [
        pltpu.make_async_remote_copy(
            st.at[1 - side, :, span(i)], r1.at[:, span(i)], s1_send.at[i], s1_recv.at[i],
            device_id=(partner, head), device_id_type=MESH,
        )
        for i in range(CHUNKS)
    ]
    for copy in first_copies:
        copy.start()

    scaled_2, grads_2 = split(scaled), split(grads)
    panels = ((0, mid), (mid, tokens))

    def part(pair, rows, columns=slice(None)):
        return tuple(x[rows, columns] for x in pair)

    inner = [
        dot3(part(read, slice(lo, hi)), part(write_t, slice(None), slice(0, hi)), 1, 0)
        for lo, hi in panels
    ]
    lanes = 2 * width
    lane = lax.broadcasted_iota(jnp.int32, (1, lanes), 1) // width
    rel_cols = jnp.concatenate([rel] * (8 // heads), axis=0).T
    out_ref[...] = jnp.zeros_like(out_ref)
    back[...] = jnp.zeros_like(back)
    wsum[...] = jnp.zeros_like(wsum)

    def near(h):
        here = slice(h // 2 * lanes, (h // 2 + 1) * lanes)
        mask = jnp.where(lane == h % 2, 1.0, 0.0).astype(BF16)
        scaled_h = tuple(x[:, here] * mask for x in scaled_2)
        grads_h = tuple(x[:, here] * mask for x in grads_2)
        for k, (lo, hi) in enumerate(panels):
            rows, reach = slice(lo, hi), slice(0, hi)
            gap = rel_cols[rows, h : h + 1] - rel[h : h + 1, reach]
            lower = row_ids[rows, reach] >= col_ids[rows, reach]
            decay = jnp.exp(jnp.where(lower, gap, -1e30))
            mixed = split(inner[k] * decay)
            out_ref[rows, here] += dot3(mixed, part(scaled_h, reach), 1, 0)
            back[reach, here] += dot3(mixed, part(grads_h, rows), 0, 0)
            wsum[rows, reach] += decay * dot3(
                part(grads_2, rows, here), part(scaled_h, reach), 1, 1
            )

    is_first = side == 0

    def rows_of(i):
        return slice(PAD + i * piece, PAD + (i + 1) * piece)

    def pair_parts(i):
        own, other = st[side, :, rows_of(i)], r1[:, rows_of(i)]
        own_decay, other_decay = st[side, 0, :PAD], r1[0, :PAD]
        return (
            jnp.where(is_first, own, other),
            jnp.where(is_first, other, own),
            spread(jnp.where(is_first, own_decay, other_decay)),
            spread(jnp.where(is_first, other_decay, own_decay)),
        )

    z_copies = []

    def send_totals(i):
        first_copies[i].wait()
        part_0, part_1, decay_0, decay_1 = pair_parts(i)
        tz[0, rows_of(i)] = decay_1 * part_0[0] + part_1[0]
        tz[1, rows_of(i)] = part_0[1] + decay_0 * part_1[1]
        if i == 0:
            for d in range(2):
                tz[d, :PAD] = decay_0[:PAD] * decay_1[:PAD]
        for k in range(1, m):
            peer_row = lax.rem(row + k, m)
            direction = jnp.where(peer_row > row, 0, 1)
            copy = pltpu.make_async_remote_copy(
                tz.at[direction, span(i)], zbuf.at[row, span(i)],
                z_send.at[i, k - 1], z_recv.at[i, row],
                device_id=(peer_row * 2 + side, head), device_id_type=MESH,
            )
            copy.start()
            z_copies.append(copy)

    last_copies = []

    def send_entering(i):
        def joined(j, carried):
            pltpu.make_async_remote_copy(
                tz.at[0, span(i)], zbuf.at[j, span(i)], z_send.at[i, 0], z_recv.at[i, j],
                device_id=(partner, head), device_id_type=MESH,
            ).wait_recv()
            return zbuf[j, rows_of(i)] + spread(zbuf[j, :PAD]) * carried

        zero = jnp.zeros((piece, half), F32)
        carry_f = lax.fori_loop(0, row, joined, zero)
        carry_b = lax.fori_loop(0, m - 1 - row, lambda k, c: joined(m - 1 - k, c), zero)
        part_0, part_1, decay_0, decay_1 = pair_parts(i)
        enter_f = (carry_f, decay_0 * carry_f + part_0[0])
        enter_b = (part_1[1] + decay_1 * carry_b, carry_b)
        for d, pair in enumerate((enter_f, enter_b)):
            fs[side, d, i * piece : (i + 1) * piece] = jnp.where(is_first, pair[0], pair[1])
            fsend[d, i * piece : (i + 1) * piece] = jnp.where(is_first, pair[1], pair[0])
        here = pl.ds(i * piece, piece)
        copy = pltpu.make_async_remote_copy(
            fsend.at[:, here], fs.at[side, :, here], s3_send.at[i], s3_recv.at[i],
            device_id=(partner, head), device_id_type=MESH,
        )
        copy.start()
        last_copies.append(copy)

    near(0)
    send_totals(0)
    near(1)
    send_totals(1)
    send_totals(2)
    near(2)
    send_totals(3)
    near(3)
    send_entering(0)
    mixed_sums = split(wsum[...])
    read_near = dot3(mixed_sums, write, 1, 0)
    write_near = dot3(mixed_sums, read, 0, 0)
    for i in range(1, CHUNKS):
        send_entering(i)
    for copy in last_copies:
        copy.wait()

    state_b = split(jnp.concatenate([fs[0, 1], fs[1, 1]], axis=1))
    state_f = split(jnp.concatenate([fs[0, 0], fs[1, 0]], axis=1))
    h_copies = []
    for which, (nearby, factor, far) in enumerate((
        (write_near, outof_s, state_b), (read_near, into_g, state_f),
    )):
        total = nearby + dot3(factor, far, 1, 1)
        for j in range(nh):
            tot[which, j] = total[j * ck : (j + 1) * ck]
        for k in range(1, nh):
            peer = lax.rem(head + k, nh)
            copy = pltpu.make_async_remote_copy(
                tot.at[which, peer], rs.at[which, k - 1],
                h_send.at[which, k - 1], h_recv.at[which, k - 1],
                device_id=(ctx, peer), device_id_type=MESH,
            )
            copy.start()
            h_copies.append(copy)

    out_ref[...] += into_w * dot3(read, state_f, 1, 0)
    back_all = back[...] + outof_w * dot3(write, state_b, 1, 0)
    gin_ref[...] = step_w * back_all
    pick_row = lax.broadcasted_iota(jnp.int32, (16, channels), 0)
    pick_col = lax.broadcasted_iota(jnp.int32, (16, channels), 1) // width
    pick = jnp.where(pick_row == pick_col, 1.0, 0.0).astype(BF16)
    high, low = split(x_ref[...] * back_all)
    nt = (((1,), (1,)), ((), ()))
    steps = lax.dot_general(pick, high, nt, preferred_element_type=F32) + lax.dot_general(
        pick, low, nt, preferred_element_type=F32
    )
    gstep_ref[...] = steps[:heads]

    for which, target in enumerate((wg_ref, rg_ref)):
        result = tot[which, head]
        for k in range(1, nh):
            h_copies[which * (nh - 1) + k - 1].wait()
            result = result + rs[which, k - 1]
        target[...] = result
    for copy in z_copies:
        copy.wait_send()


def place(*refs):
    count = len(refs) // 2
    sems = refs[-1]
    copies = [
        pltpu.make_async_copy(refs[i], refs[count + i], sems.at[i]) for i in range(count)
    ]
    for copy in copies:
        copy.start()
    for copy in copies:
        copy.wait()


def solution(mesh):
    n, nh = mesh.shape["ctx"], mesh.shape["head"]
    m = n // 2

    def shards(head_input, step_size, log_decay, write_proj, read_proj, grad_out):
        tokens, channels = head_input.shape
        heads = step_size.shape[0]
        state = write_proj.shape[1]
        half, ck = channels // 2, tokens // nh
        vmem = pl.BlockSpec(memory_space=pltpu.VMEM)
        hbm = pl.BlockSpec(memory_space=pltpu.HBM)
        dma = pltpu.SemaphoreType.DMA
        shapes = (
            jax.ShapeDtypeStruct((tokens, channels), F32),
            jax.ShapeDtypeStruct((tokens, channels), F32),
            jax.ShapeDtypeStruct((heads, tokens), F32),
            jax.ShapeDtypeStruct((ck, state), F32),
            jax.ShapeDtypeStruct((ck, state), F32),
        )
        results = pl.pallas_call(
            functools.partial(kernel, n, nh),
            out_shape=tuple(pltpu.VMEM(shape.shape, F32) for shape in shapes),
            in_specs=[hbm] * 6,
            out_specs=(vmem,) * 5,
            scratch_shapes=[
                pltpu.VMEM((tokens, channels), F32),
                pltpu.VMEM((heads, tokens), F32),
                pltpu.VMEM((heads, tokens), F32),
                pltpu.VMEM((tokens, state), F32),
                pltpu.VMEM((tokens, state), F32),
                pltpu.VMEM((tokens, channels), F32),
                pltpu.VMEM((2, 2, state + PAD, half), F32),
                pltpu.VMEM((2, state + PAD, half), F32),
                pltpu.VMEM((2, state + PAD, half), F32),
                pltpu.VMEM((m, state + PAD, half), F32),
                pltpu.VMEM((2, state, half), F32),
                pltpu.VMEM((2, 2, state, half), F32),
                pltpu.VMEM((2, nh, ck, state), F32),
                pltpu.VMEM((2, nh - 1, ck, state), F32),
                pltpu.VMEM((tokens, tokens), F32),
                pltpu.VMEM((tokens, channels), F32),
                dma((6,)),
                dma((CHUNKS,)), dma((CHUNKS,)),
                dma((CHUNKS, m - 1)), dma((CHUNKS, m)),
                dma((CHUNKS,)), dma((CHUNKS,)),
                dma((2, nh - 1)), dma((2, nh - 1)),
            ],
            compiler_params=pltpu.CompilerParams(
                collective_id=0, has_side_effects=True, vmem_limit_bytes=GRANT
            ),
        )(*(
            pltpu.with_memory_space_constraint(x, pltpu.HBM)
            for x in (head_input, step_size, log_decay, write_proj, read_proj, grad_out)
        ))
        return pl.pallas_call(
            place,
            out_shape=shapes,
            in_specs=[vmem] * 5,
            out_specs=(hbm,) * 5,
            scratch_shapes=[dma((5,))],
        )(*results)

    return jax.shard_map(
        shards,
        mesh=mesh,
        in_specs=(
            P("ctx", "head"), P("head", "ctx"), P("head", "ctx"),
            P("ctx", None), P("ctx", None), P("ctx", "head"),
        ),
        out_specs=(
            P("ctx", "head"), P("ctx", "head"), P("head", "ctx"),
            P(("ctx", "head"), None), P(("ctx", "head"), None),
        ),
        check_vma=False,
    )
```

```python
import functools

import jax
import jax.numpy as jnp
from jax import lax
from jax.experimental import pallas as pl
from jax.experimental.pallas import tpu as pltpu
from jax.sharding import PartitionSpec as P

MESH = pl.DeviceIdType.MESH
F32 = jnp.float32
BF16 = jnp.bfloat16
PAD = 8
GRANT = 32 * 2**20
CHUNKS = 4


def split(x):
    high = x.astype(BF16)
    return high, (x - high.astype(F32)).astype(BF16)


def dot3(a, b, ca, cb):
    left = jnp.concatenate([a[0], a[0], a[1]], axis=ca)
    right = jnp.concatenate([b[0], b[1], b[0]], axis=cb)
    return lax.dot_general(left, right, (((ca,), (cb,)), ((), ())), preferred_element_type=F32)


def thirds(rows):
    zeros = jnp.zeros((16 - rows.shape[0], rows.shape[1]), F32)
    pieces = []
    for _ in range(3):
        piece = rows.astype(BF16)
        rows = rows - piece.astype(F32)
        pieces.append(jnp.concatenate([piece.astype(F32), zeros], axis=0))
    return jnp.concatenate(pieces, axis=0).astype(BF16)


def kernel(
    n, nh,
    x_hbm, step_hbm, log_hbm, b_hbm, c_hbm, g_hbm,
    out_ref, gin_ref, gstep_ref, wg_ref, rg_ref,
    x_ref, step_ref, log_ref, b_ref, c_ref, g_ref,
    st, r1, tz, zbuf, fsend, fs, tot, rs, wsum, back,
    in_sem, s1_send, s1_recv, z_send, z_recv, s3_send, s3_recv, h_send, h_recv,
):
    tokens, channels = x_ref.shape
    heads = step_ref.shape[0]
    width = channels // heads
    state = b_ref.shape[1]
    half = channels // 2
    m = n // 2
    ck = tokens // nh
    piece = state // CHUNKS

    ctx, head = lax.axis_index("ctx"), lax.axis_index("head")
    side, row = lax.rem(ctx, 2), lax.div(ctx, 2)
    partner = row * 2 + (1 - side)

    barrier = pltpu.get_barrier_semaphore()
    pl.semaphore_signal(barrier, inc=1, device_id=(partner, head), device_id_type=MESH)
    for k in range(1, m):
        peer = lax.rem(row + k, m) * 2 + side
        pl.semaphore_signal(barrier, inc=1, device_id=(peer, head), device_id_type=MESH)
    for k in range(1, nh):
        pl.semaphore_signal(
            barrier, inc=1, device_id=(ctx, lax.rem(head + k, nh)), device_id_type=MESH
        )

    loads = [
        pltpu.make_async_copy(source, target, in_sem.at[i])
        for i, (source, target) in enumerate((
            (log_hbm, log_ref), (step_hbm, step_ref), (b_hbm, b_ref),
            (c_hbm, c_ref), (x_hbm, x_ref), (g_hbm, g_ref),
        ))
    ]
    for load in loads:
        load.start()

    mid = tokens // 2
    row_ids = lax.broadcasted_iota(jnp.int32, (tokens, tokens), 0)
    col_ids = lax.broadcasted_iota(jnp.int32, (tokens, tokens), 1)
    weights = jnp.where(
        (row_ids <= col_ids) & (row_ids >= mid),
        1.0,
        jnp.where((row_ids > col_ids) & (row_ids < mid), -1.0, 0.0),
    ).astype(BF16)
    pick_row = lax.broadcasted_iota(jnp.int32, (48, 3 * channels), 0) % 16
    pick_col = lax.broadcasted_iota(jnp.int32, (48, 3 * channels), 1) // width
    expand = jnp.where(pick_row == pick_col, 1.0, 0.0).astype(BF16)

    loads[0].wait()
    logs = log_ref[...]
    sums = jnp.dot(thirds(logs), weights, preferred_element_type=F32)
    rel = sums[:heads] + sums[16 : 16 + heads] + sums[32 : 32 + heads]
    before = jnp.sum(logs[:, :mid], axis=1, keepdims=True)
    last = rel[:, tokens - 1 : tokens]
    into = jnp.exp(rel + before)
    outof = jnp.exp(last - rel)
    loads[1].wait()
    factors = thirds(jnp.concatenate([step_ref[...], into, outof], axis=0))
    wide = lax.dot_general(
        factors, expand, (((0,), (0,)), ((), ())), preferred_element_type=F32
    )
    step_w = wide[:, :channels]
    into_w = wide[:, channels : 2 * channels]
    outof_w = wide[:, 2 * channels :]

    loads[2].wait()
    write, write_t = split(b_ref[...]), split(b_ref[...].T)
    loads[3].wait()
    read, read_t = split(c_ref[...]), split(c_ref[...].T)
    loads[4].wait()
    scaled = x_ref[...] * step_w
    outof_s = split(outof_w * scaled)
    fwd = dot3(write_t, outof_s, 1, 0)
    loads[5].wait()
    grads = g_ref[...]
    into_g = split(into_w * grads)
    bwd = dot3(read_t, into_g, 1, 0)
    decay_rows = jnp.broadcast_to(into_w[tokens - 1 : tokens], (PAD, channels))
    for j in range(2):
        for d, whole in enumerate((fwd, bwd)):
            st[j, d, :PAD] = decay_rows[:, j * half : (j + 1) * half]
            st[j, d, PAD:] = whole[:, j * half : (j + 1) * half]

    def span(i):
        return pl.ds(0, PAD + piece) if i == 0 else pl.ds(PAD + i * piece, piece)

    def spread(decay):
        return jnp.concatenate([decay] * (piece // PAD), axis=0)

    pl.semaphore_wait(barrier, 1 + (m - 1) + (nh - 1))
    first_copies = [
        pltpu.make_async_remote_copy(
            st.at[1 - side, :, span(i)], r1.at[:, span(i)], s1_send.at[i], s1_recv.at[i],
            device_id=(partner, head), device_id_type=MESH,
        )
        for i in range(CHUNKS)
    ]
    for copy in first_copies:
        copy.start()

    scaled_2, grads_2 = split(scaled), split(grads)
    panels = ((0, mid), (mid, tokens))

    def part(pair, rows, columns=slice(None)):
        return tuple(x[rows, columns] for x in pair)

    inner = [
        dot3(part(read, slice(lo, hi)), part(write_t, slice(None), slice(0, hi)), 1, 0)
        for lo, hi in panels
    ]
    lanes = 2 * width
    lane = lax.broadcasted_iota(jnp.int32, (1, lanes), 1) // width
    rel_cols = jnp.concatenate([rel] * (8 // heads), axis=0).T
    out_ref[...] = jnp.zeros_like(out_ref)
    back[...] = jnp.zeros_like(back)
    wsum[...] = jnp.zeros_like(wsum)

    def near(h):
        here = slice(h // 2 * lanes, (h // 2 + 1) * lanes)
        mask = jnp.where(lane == h % 2, 1.0, 0.0).astype(BF16)
        scaled_h = tuple(x[:, here] * mask for x in scaled_2)
        grads_h = tuple(x[:, here] * mask for x in grads_2)
        for k, (lo, hi) in enumerate(panels):
            rows, reach = slice(lo, hi), slice(0, hi)
            gap = rel_cols[rows, h : h + 1] - rel[h : h + 1, reach]
            lower = row_ids[rows, reach] >= col_ids[rows, reach]
            decay = jnp.exp(jnp.where(lower, gap, -1e30))
            mixed = split(inner[k] * decay)
            out_ref[rows, here] += dot3(mixed, part(scaled_h, reach), 1, 0)
            back[reach, here] += dot3(mixed, part(grads_h, rows), 0, 0)
            wsum[rows, reach] += decay * dot3(
                part(grads_2, rows, here), part(scaled_h, reach), 1, 1
            )

    is_first = side == 0

    def rows_of(i):
        return slice(PAD + i * piece, PAD + (i + 1) * piece)

    def pair_parts(i):
        own, other = st[side, :, rows_of(i)], r1[:, rows_of(i)]
        own_decay, other_decay = st[side, 0, :PAD], r1[0, :PAD]
        return (
            jnp.where(is_first, own, other),
            jnp.where(is_first, other, own),
            spread(jnp.where(is_first, own_decay, other_decay)),
            spread(jnp.where(is_first, other_decay, own_decay)),
        )

    z_copies = []

    def send_totals(i):
        first_copies[i].wait()
        part_0, part_1, decay_0, decay_1 = pair_parts(i)
        tz[0, rows_of(i)] = decay_1 * part_0[0] + part_1[0]
        tz[1, rows_of(i)] = part_0[1] + decay_0 * part_1[1]
        if i == 0:
            for d in range(2):
                tz[d, :PAD] = decay_0[:PAD] * decay_1[:PAD]
        for k in range(1, m):
            peer_row = lax.rem(row + k, m)
            direction = jnp.where(peer_row > row, 0, 1)
            copy = pltpu.make_async_remote_copy(
                tz.at[direction, span(i)], zbuf.at[row, span(i)],
                z_send.at[i, k - 1], z_recv.at[i, row],
                device_id=(peer_row * 2 + side, head), device_id_type=MESH,
            )
            copy.start()
            z_copies.append(copy)

    last_copies = []

    def send_entering(i):
        def joined(j, carried):
            pltpu.make_async_remote_copy(
                tz.at[0, span(i)], zbuf.at[j, span(i)], z_send.at[i, 0], z_recv.at[i, j],
                device_id=(partner, head), device_id_type=MESH,
            ).wait_recv()
            return zbuf[j, rows_of(i)] + spread(zbuf[j, :PAD]) * carried

        zero = jnp.zeros((piece, half), F32)
        carry_f = lax.fori_loop(0, row, joined, zero)
        carry_b = lax.fori_loop(0, m - 1 - row, lambda k, c: joined(m - 1 - k, c), zero)
        part_0, part_1, decay_0, decay_1 = pair_parts(i)
        enter_f = (carry_f, decay_0 * carry_f + part_0[0])
        enter_b = (part_1[1] + decay_1 * carry_b, carry_b)
        for d, pair in enumerate((enter_f, enter_b)):
            fs[side, d, i * piece : (i + 1) * piece] = jnp.where(is_first, pair[0], pair[1])
            fsend[d, i * piece : (i + 1) * piece] = jnp.where(is_first, pair[1], pair[0])
        here = pl.ds(i * piece, piece)
        copy = pltpu.make_async_remote_copy(
            fsend.at[:, here], fs.at[side, :, here], s3_send.at[i], s3_recv.at[i],
            device_id=(partner, head), device_id_type=MESH,
        )
        copy.start()
        last_copies.append(copy)

    near(0)
    send_totals(0)
    near(1)
    send_totals(1)
    send_totals(2)
    near(2)
    send_totals(3)
    near(3)
    send_entering(0)
    mixed_sums = split(wsum[...])
    read_near = dot3(mixed_sums, write, 1, 0)
    write_near = dot3(mixed_sums, read, 0, 0)
    for i in range(1, CHUNKS):
        send_entering(i)
    for copy in last_copies:
        copy.wait()

    state_b = split(jnp.concatenate([fs[0, 1], fs[1, 1]], axis=1))
    state_f = split(jnp.concatenate([fs[0, 0], fs[1, 0]], axis=1))
    h_copies = []
    for which, (nearby, factor, far) in enumerate((
        (write_near, outof_s, state_b), (read_near, into_g, state_f),
    )):
        total = nearby + dot3(factor, far, 1, 1)
        for j in range(nh):
            tot[which, j] = total[j * ck : (j + 1) * ck]
        for k in range(1, nh):
            peer = lax.rem(head + k, nh)
            copy = pltpu.make_async_remote_copy(
                tot.at[which, peer], rs.at[which, k - 1],
                h_send.at[which, k - 1], h_recv.at[which, k - 1],
                device_id=(ctx, peer), device_id_type=MESH,
            )
            copy.start()
            h_copies.append(copy)

    out_ref[...] += into_w * dot3(read, state_f, 1, 0)
    back_all = back[...] + outof_w * dot3(write, state_b, 1, 0)
    gin_ref[...] = step_w * back_all
    pick_row = lax.broadcasted_iota(jnp.int32, (16, channels), 0)
    pick_col = lax.broadcasted_iota(jnp.int32, (16, channels), 1) // width
    pick = jnp.where(pick_row == pick_col, 1.0, 0.0).astype(BF16)
    high, low = split(x_ref[...] * back_all)
    nt = (((1,), (1,)), ((), ()))
    steps = lax.dot_general(pick, high, nt, preferred_element_type=F32) + lax.dot_general(
        pick, low, nt, preferred_element_type=F32
    )
    gstep_ref[...] = steps[:heads]

    for which, target in enumerate((wg_ref, rg_ref)):
        result = tot[which, head]
        for k in range(1, nh):
            h_copies[which * (nh - 1) + k - 1].wait()
            result = result + rs[which, k - 1]
        target[...] = result
    for copy in z_copies:
        copy.wait_send()


def place(*refs):
    count = len(refs) // 2
    sems = refs[-1]
    copies = [
        pltpu.make_async_copy(refs[i], refs[count + i], sems.at[i]) for i in range(count)
    ]
    for copy in copies:
        copy.start()
    for copy in copies:
        copy.wait()


def solution(mesh):
    n, nh = mesh.shape["ctx"], mesh.shape["head"]
    m = n // 2

    def shards(head_input, step_size, log_decay, write_proj, read_proj, grad_out):
        tokens, channels = head_input.shape
        heads = step_size.shape[0]
        state = write_proj.shape[1]
        half, ck = channels // 2, tokens // nh
        vmem = pl.BlockSpec(memory_space=pltpu.VMEM)
        hbm = pl.BlockSpec(memory_space=pltpu.HBM)
        dma = pltpu.SemaphoreType.DMA
        shapes = (
            jax.ShapeDtypeStruct((tokens, channels), F32),
            jax.ShapeDtypeStruct((tokens, channels), F32),
            jax.ShapeDtypeStruct((heads, tokens), F32),
            jax.ShapeDtypeStruct((ck, state), F32),
            jax.ShapeDtypeStruct((ck, state), F32),
        )
        results = pl.pallas_call(
            functools.partial(kernel, n, nh),
            out_shape=tuple(pltpu.VMEM(shape.shape, F32) for shape in shapes),
            in_specs=[hbm] * 6,
            out_specs=(vmem,) * 5,
            scratch_shapes=[
                pltpu.VMEM((tokens, channels), F32),
                pltpu.VMEM((heads, tokens), F32),
                pltpu.VMEM((heads, tokens), F32),
                pltpu.VMEM((tokens, state), F32),
                pltpu.VMEM((tokens, state), F32),
                pltpu.VMEM((tokens, channels), F32),
                pltpu.VMEM((2, 2, state + PAD, half), F32),
                pltpu.VMEM((2, state + PAD, half), F32),
                pltpu.VMEM((2, state + PAD, half), F32),
                pltpu.VMEM((m, state + PAD, half), F32),
                pltpu.VMEM((2, state, half), F32),
                pltpu.VMEM((2, 2, state, half), F32),
                pltpu.VMEM((2, nh, ck, state), F32),
                pltpu.VMEM((2, nh - 1, ck, state), F32),
                pltpu.VMEM((tokens, tokens), F32),
                pltpu.VMEM((tokens, channels), F32),
                dma((6,)),
                dma((CHUNKS,)), dma((CHUNKS,)),
                dma((CHUNKS, m - 1)), dma((CHUNKS, m)),
                dma((CHUNKS,)), dma((CHUNKS,)),
                dma((2, nh - 1)), dma((2, nh - 1)),
            ],
            compiler_params=pltpu.CompilerParams(
                collective_id=0, has_side_effects=True, vmem_limit_bytes=GRANT
            ),
        )(*(
            pltpu.with_memory_space_constraint(x, pltpu.HBM)
            for x in (head_input, step_size, log_decay, write_proj, read_proj, grad_out)
        ))
        return pl.pallas_call(
            place,
            out_shape=shapes,
            in_specs=[vmem] * 5,
            out_specs=(hbm,) * 5,
            scratch_shapes=[dma((5,))],
            compiler_params=pltpu.CompilerParams(vmem_limit_bytes=4 * 2**20),
        )(*(pltpu.with_memory_space_constraint(x, pltpu.VMEM) for x in results))

    return jax.shard_map(
        shards,
        mesh=mesh,
        in_specs=(
            P("ctx", "head"), P("head", "ctx"), P("head", "ctx"),
            P("ctx", None), P("ctx", None), P("ctx", "head"),
        ),
        out_specs=(
            P("ctx", "head"), P("ctx", "head"), P("head", "ctx"),
            P(("ctx", "head"), None), P(("ctx", "head"), None),
        ),
        check_vma=False,
    )
```

```python
import functools

import jax
import jax.numpy as jnp
from jax import lax
from jax.experimental import pallas as pl
from jax.experimental.pallas import tpu as pltpu
from jax.sharding import PartitionSpec as P

MESH = pl.DeviceIdType.MESH
F32 = jnp.float32
BF16 = jnp.bfloat16
PAD = 8
GRANT = 32 * 2**20
CHUNKS = 4


def split(x):
    high = x.astype(BF16)
    return high, (x - high.astype(F32)).astype(BF16)


def dot3(a, b, ca, cb):
    left = jnp.concatenate([a[0], a[0], a[1]], axis=ca)
    right = jnp.concatenate([b[0], b[1], b[0]], axis=cb)
    return lax.dot_general(left, right, (((ca,), (cb,)), ((), ())), preferred_element_type=F32)


def thirds(rows):
    zeros = jnp.zeros((16 - rows.shape[0], rows.shape[1]), F32)
    pieces = []
    for _ in range(3):
        piece = rows.astype(BF16)
        rows = rows - piece.astype(F32)
        pieces.append(jnp.concatenate([piece.astype(F32), zeros], axis=0))
    return jnp.concatenate(pieces, axis=0).astype(BF16)


def kernel(
    n, nh,
    x_hbm, step_hbm, log_hbm, b_hbm, c_hbm, g_hbm,
    out_ref, gin_ref, gstep_ref, wg_ref, rg_ref,
    x_ref, step_ref, log_ref, b_ref, c_ref, g_ref,
    st, r1, tz, za, gz, zbuf, fsend, fs, tot, rs, wsum, back,
    in_sem, s1_send, s1_recv, a_send, a_recv, z_send, z_recv, s3_send, s3_recv, h_send, h_recv,
):
    tokens, channels = x_ref.shape
    heads = step_ref.shape[0]
    width = channels // heads
    state = b_ref.shape[1]
    half = channels // 2
    m = n // 2
    ck = tokens // nh
    piece = state // CHUNKS

    ctx, head = lax.axis_index("ctx"), lax.axis_index("head")
    side, row = lax.rem(ctx, 2), lax.div(ctx, 2)
    partner = row * 2 + (1 - side)
    rank, group, groups = lax.rem(row, 2), lax.div(row, 2), m // 2
    mate = (row + 1 - 2 * rank) * 2 + side

    barrier = pltpu.get_barrier_semaphore()
    pl.semaphore_signal(barrier, inc=1, device_id=(partner, head), device_id_type=MESH)
    for k in range(1, m):
        peer = lax.rem(row + k, m) * 2 + side
        pl.semaphore_signal(barrier, inc=1, device_id=(peer, head), device_id_type=MESH)
    for k in range(1, nh):
        pl.semaphore_signal(
            barrier, inc=1, device_id=(ctx, lax.rem(head + k, nh)), device_id_type=MESH
        )

    loads = [
        pltpu.make_async_copy(source, target, in_sem.at[i])
        for i, (source, target) in enumerate((
            (log_hbm, log_ref), (step_hbm, step_ref), (b_hbm, b_ref),
            (c_hbm, c_ref), (x_hbm, x_ref), (g_hbm, g_ref),
        ))
    ]
    for load in loads:
        load.start()

    mid = tokens // 2
    row_ids = lax.broadcasted_iota(jnp.int32, (tokens, tokens), 0)
    col_ids = lax.broadcasted_iota(jnp.int32, (tokens, tokens), 1)
    weights = jnp.where(
        (row_ids <= col_ids) & (row_ids >= mid),
        1.0,
        jnp.where((row_ids > col_ids) & (row_ids < mid), -1.0, 0.0),
    ).astype(BF16)
    pick_row = lax.broadcasted_iota(jnp.int32, (48, 3 * channels), 0) % 16
    pick_col = lax.broadcasted_iota(jnp.int32, (48, 3 * channels), 1) // width
    expand = jnp.where(pick_row == pick_col, 1.0, 0.0).astype(BF16)

    loads[0].wait()
    logs = log_ref[...]
    sums = jnp.dot(thirds(logs), weights, preferred_element_type=F32)
    rel = sums[:heads] + sums[16 : 16 + heads] + sums[32 : 32 + heads]
    before = jnp.sum(logs[:, :mid], axis=1, keepdims=True)
    last = rel[:, tokens - 1 : tokens]
    into = jnp.exp(rel + before)
    outof = jnp.exp(last - rel)
    loads[1].wait()
    factors = thirds(jnp.concatenate([step_ref[...], into, outof], axis=0))
    wide = lax.dot_general(
        factors, expand, (((0,), (0,)), ((), ())), preferred_element_type=F32
    )
    step_w = wide[:, :channels]
    into_w = wide[:, channels : 2 * channels]
    outof_w = wide[:, 2 * channels :]

    loads[2].wait()
    write, write_t = split(b_ref[...]), split(b_ref[...].T)
    loads[3].wait()
    read, read_t = split(c_ref[...]), split(c_ref[...].T)
    loads[4].wait()
    scaled = x_ref[...] * step_w
    outof_s = split(outof_w * scaled)
    fwd = dot3(write_t, outof_s, 1, 0)
    loads[5].wait()
    grads = g_ref[...]
    into_g = split(into_w * grads)
    bwd = dot3(read_t, into_g, 1, 0)
    decay_rows = jnp.broadcast_to(into_w[tokens - 1 : tokens], (PAD, channels))
    for j in range(2):
        for d, whole in enumerate((fwd, bwd)):
            st[j, d, :PAD] = decay_rows[:, j * half : (j + 1) * half]
            st[j, d, PAD:] = whole[:, j * half : (j + 1) * half]

    def span(i):
        return pl.ds(0, PAD + piece) if i == 0 else pl.ds(PAD + i * piece, piece)

    def spread(decay):
        return jnp.concatenate([decay] * (piece // PAD), axis=0)

    pl.semaphore_wait(barrier, 1 + (m - 1) + (nh - 1))
    first_copies = [
        pltpu.make_async_remote_copy(
            st.at[1 - side, :, span(i)], r1.at[:, span(i)], s1_send.at[i], s1_recv.at[i],
            device_id=(partner, head), device_id_type=MESH,
        )
        for i in range(CHUNKS)
    ]
    for copy in first_copies:
        copy.start()

    scaled_2, grads_2 = split(scaled), split(grads)
    panels = ((0, mid), (mid, tokens))

    def part(pair, rows, columns=slice(None)):
        return tuple(x[rows, columns] for x in pair)

    inner = [
        dot3(part(read, slice(lo, hi)), part(write_t, slice(None), slice(0, hi)), 1, 0)
        for lo, hi in panels
    ]
    lanes = 2 * width
    lane = lax.broadcasted_iota(jnp.int32, (1, lanes), 1) // width
    rel_cols = jnp.concatenate([rel] * (8 // heads), axis=0).T
    out_ref[...] = jnp.zeros_like(out_ref)
    back[...] = jnp.zeros_like(back)
    wsum[...] = jnp.zeros_like(wsum)

    def near(h):
        here = slice(h // 2 * lanes, (h // 2 + 1) * lanes)
        mask = jnp.where(lane == h % 2, 1.0, 0.0).astype(BF16)
        scaled_h = tuple(x[:, here] * mask for x in scaled_2)
        grads_h = tuple(x[:, here] * mask for x in grads_2)
        for k, (lo, hi) in enumerate(panels):
            rows, reach = slice(lo, hi), slice(0, hi)
            gap = rel_cols[rows, h : h + 1] - rel[h : h + 1, reach]
            lower = row_ids[rows, reach] >= col_ids[rows, reach]
            decay = jnp.exp(jnp.where(lower, gap, -1e30))
            mixed = split(inner[k] * decay)
            out_ref[rows, here] += dot3(mixed, part(scaled_h, reach), 1, 0)
            back[reach, here] += dot3(mixed, part(grads_h, rows), 0, 0)
            wsum[rows, reach] += decay * dot3(
                part(grads_2, rows, here), part(scaled_h, reach), 1, 1
            )

    is_first = side == 0

    def rows_of(i):
        return slice(PAD + i * piece, PAD + (i + 1) * piece)

    def pair_parts(i):
        own, other = st[side, :, rows_of(i)], r1[:, rows_of(i)]
        own_decay, other_decay = st[side, 0, :PAD], r1[0, :PAD]
        return (
            jnp.where(is_first, own, other),
            jnp.where(is_first, other, own),
            spread(jnp.where(is_first, own_decay, other_decay)),
            spread(jnp.where(is_first, other_decay, own_decay)),
        )

    mate_copies = []

    def send_totals(i):
        first_copies[i].wait()
        part_0, part_1, decay_0, decay_1 = pair_parts(i)
        tz[0, rows_of(i)] = decay_1 * part_0[0] + part_1[0]
        tz[1, rows_of(i)] = part_0[1] + decay_0 * part_1[1]
        if i == 0:
            for d in range(2):
                tz[d, :PAD] = decay_0[:PAD] * decay_1[:PAD]
        copy = pltpu.make_async_remote_copy(
            tz.at[rank, span(i)], za.at[span(i)], a_send.at[i], a_recv.at[i],
            device_id=(mate, head), device_id_type=MESH,
        )
        copy.start()
        mate_copies.append(copy)

    def group_copies(act):
        for k in range(1, groups):
            other = lax.rem(group + k, groups)

            @pl.when(jnp.where(other > group, 1, 0) == rank)
            def _():
                for r in range(2):
                    act(k, r, (other * 2 + r) * 2 + side)

    def group_copy(i, k, r, peer):
        return pltpu.make_async_remote_copy(
            gz.at[span(i)], zbuf.at[group, span(i)],
            z_send.at[i, 2 * (k - 1) + r], z_recv.at[i, group],
            device_id=(peer, head), device_id_type=MESH,
        )

    def send_groups(i):
        mate_copies[i].wait()
        own_decay, mate_decay = tz[0, :PAD], za[:PAD]
        gz[rows_of(i)] = tz[1 - rank, rows_of(i)] + spread(own_decay) * za[rows_of(i)]
        if i == 0:
            gz[:PAD] = own_decay * mate_decay
        group_copies(lambda k, r, peer: group_copy(i, k, r, peer).start())

    last_copies = []

    def send_entering(i):
        def joined(j, carried):
            pltpu.make_async_remote_copy(
                gz.at[span(i)], zbuf.at[j, span(i)], z_send.at[i, 0], z_recv.at[i, j],
                device_id=(partner, head), device_id_type=MESH,
            ).wait_recv()
            return zbuf[j, rows_of(i)] + spread(zbuf[j, :PAD]) * carried

        zero = jnp.zeros((piece, half), F32)
        carry_f = lax.fori_loop(0, group, joined, zero)
        carry_b = lax.fori_loop(
            0, groups - 1 - group, lambda k, c: joined(groups - 1 - k, c), zero
        )
        mate_part, mate_decay = za[rows_of(i)], spread(za[:PAD])
        carry_f = jnp.where(rank == 1, mate_part + mate_decay * carry_f, carry_f)
        carry_b = jnp.where(rank == 0, mate_part + mate_decay * carry_b, carry_b)
        part_0, part_1, decay_0, decay_1 = pair_parts(i)
        enter_f = (carry_f, decay_0 * carry_f + part_0[0])
        enter_b = (part_1[1] + decay_1 * carry_b, carry_b)
        for d, pair in enumerate((enter_f, enter_b)):
            fs[side, d, i * piece : (i + 1) * piece] = jnp.where(is_first, pair[0], pair[1])
            fsend[d, i * piece : (i + 1) * piece] = jnp.where(is_first, pair[1], pair[0])
        here = pl.ds(i * piece, piece)
        copy = pltpu.make_async_remote_copy(
            fsend.at[:, here], fs.at[side, :, here], s3_send.at[i], s3_recv.at[i],
            device_id=(partner, head), device_id_type=MESH,
        )
        copy.start()
        last_copies.append(copy)

    near(0)
    near(1)
    send_totals(0)
    send_totals(1)
    send_totals(2)
    send_groups(0)
    send_totals(3)
    send_groups(1)
    near(2)
    send_groups(2)
    send_groups(3)
    send_entering(0)
    near(3)
    send_entering(1)
    mixed_sums = split(wsum[...])
    read_near = dot3(mixed_sums, write, 1, 0)
    write_near = dot3(mixed_sums, read, 0, 0)
    for i in range(2, CHUNKS):
        send_entering(i)
    for copy in last_copies:
        copy.wait()

    state_b = split(jnp.concatenate([fs[0, 1], fs[1, 1]], axis=1))
    state_f = split(jnp.concatenate([fs[0, 0], fs[1, 0]], axis=1))
    h_copies = []
    for which, (nearby, factor, far) in enumerate((
        (write_near, outof_s, state_b), (read_near, into_g, state_f),
    )):
        total = nearby + dot3(factor, far, 1, 1)
        for j in range(nh):
            tot[which, j] = total[j * ck : (j + 1) * ck]
        for k in range(1, nh):
            peer = lax.rem(head + k, nh)
            copy = pltpu.make_async_remote_copy(
                tot.at[which, peer], rs.at[which, k - 1],
                h_send.at[which, k - 1], h_recv.at[which, k - 1],
                device_id=(ctx, peer), device_id_type=MESH,
            )
            copy.start()
            h_copies.append(copy)

    out_ref[...] += into_w * dot3(read, state_f, 1, 0)
    back_all = back[...] + outof_w * dot3(write, state_b, 1, 0)
    gin_ref[...] = step_w * back_all
    pick_row = lax.broadcasted_iota(jnp.int32, (16, channels), 0)
    pick_col = lax.broadcasted_iota(jnp.int32, (16, channels), 1) // width
    pick = jnp.where(pick_row == pick_col, 1.0, 0.0).astype(BF16)
    high, low = split(x_ref[...] * back_all)
    nt = (((1,), (1,)), ((), ()))
    steps = lax.dot_general(pick, high, nt, preferred_element_type=F32) + lax.dot_general(
        pick, low, nt, preferred_element_type=F32
    )
    gstep_ref[...] = steps[:heads]

    for which, target in enumerate((wg_ref, rg_ref)):
        result = tot[which, head]
        for k in range(1, nh):
            h_copies[which * (nh - 1) + k - 1].wait()
            result = result + rs[which, k - 1]
        target[...] = result
    for i in range(CHUNKS):
        group_copies(lambda k, r, peer: group_copy(i, k, r, peer).wait_send())


def place(*refs):
    count = len(refs) // 2
    sems = refs[-1]
    copies = [
        pltpu.make_async_copy(refs[i], refs[count + i], sems.at[i]) for i in range(count)
    ]
    for copy in copies:
        copy.start()
    for copy in copies:
        copy.wait()


def solution(mesh):
    n, nh = mesh.shape["ctx"], mesh.shape["head"]
    m = n // 2

    def shards(head_input, step_size, log_decay, write_proj, read_proj, grad_out):
        tokens, channels = head_input.shape
        heads = step_size.shape[0]
        state = write_proj.shape[1]
        half, ck = channels // 2, tokens // nh
        vmem = pl.BlockSpec(memory_space=pltpu.VMEM)
        hbm = pl.BlockSpec(memory_space=pltpu.HBM)
        dma = pltpu.SemaphoreType.DMA
        shapes = (
            jax.ShapeDtypeStruct((tokens, channels), F32),
            jax.ShapeDtypeStruct((tokens, channels), F32),
            jax.ShapeDtypeStruct((heads, tokens), F32),
            jax.ShapeDtypeStruct((ck, state), F32),
            jax.ShapeDtypeStruct((ck, state), F32),
        )
        results = pl.pallas_call(
            functools.partial(kernel, n, nh),
            out_shape=tuple(pltpu.VMEM(shape.shape, F32) for shape in shapes),
            in_specs=[hbm] * 6,
            out_specs=(vmem,) * 5,
            scratch_shapes=[
                pltpu.VMEM((tokens, channels), F32),
                pltpu.VMEM((heads, tokens), F32),
                pltpu.VMEM((heads, tokens), F32),
                pltpu.VMEM((tokens, state), F32),
                pltpu.VMEM((tokens, state), F32),
                pltpu.VMEM((tokens, channels), F32),
                pltpu.VMEM((2, 2, state + PAD, half), F32),
                pltpu.VMEM((2, state + PAD, half), F32),
                pltpu.VMEM((2, state + PAD, half), F32),
                pltpu.VMEM((state + PAD, half), F32),
                pltpu.VMEM((state + PAD, half), F32),
                pltpu.VMEM((m // 2, state + PAD, half), F32),
                pltpu.VMEM((2, state, half), F32),
                pltpu.VMEM((2, 2, state, half), F32),
                pltpu.VMEM((2, nh, ck, state), F32),
                pltpu.VMEM((2, nh - 1, ck, state), F32),
                pltpu.VMEM((tokens, tokens), F32),
                pltpu.VMEM((tokens, channels), F32),
                dma((6,)),
                dma((CHUNKS,)), dma((CHUNKS,)),
                dma((CHUNKS,)), dma((CHUNKS,)),
                dma((CHUNKS, m - 2)), dma((CHUNKS, m // 2)),
                dma((CHUNKS,)), dma((CHUNKS,)),
                dma((2, nh - 1)), dma((2, nh - 1)),
            ],
            compiler_params=pltpu.CompilerParams(
                collective_id=0, has_side_effects=True, vmem_limit_bytes=GRANT
            ),
        )(*(
            pltpu.with_memory_space_constraint(x, pltpu.HBM)
            for x in (head_input, step_size, log_decay, write_proj, read_proj, grad_out)
        ))
        return pl.pallas_call(
            place,
            out_shape=shapes,
            in_specs=[vmem] * 5,
            out_specs=(hbm,) * 5,
            scratch_shapes=[dma((5,))],
            compiler_params=pltpu.CompilerParams(vmem_limit_bytes=4 * 2**20),
        )(*(pltpu.with_memory_space_constraint(x, pltpu.VMEM) for x in results))

    return jax.shard_map(
        shards,
        mesh=mesh,
        in_specs=(
            P("ctx", "head"), P("head", "ctx"), P("head", "ctx"),
            P("ctx", None), P("ctx", None), P("ctx", "head"),
        ),
        out_specs=(
            P("ctx", "head"), P("ctx", "head"), P("head", "ctx"),
            P(("ctx", "head"), None), P(("ctx", "head"), None),
        ),
        check_vma=False,
    )
```

```python
import functools

import jax
import jax.numpy as jnp
from jax import lax
from jax.experimental import pallas as pl
from jax.experimental.pallas import tpu as pltpu
from jax.sharding import PartitionSpec as P

MESH = pl.DeviceIdType.MESH
F32 = jnp.float32
BF16 = jnp.bfloat16
PAD = 8
GRANT = 32 * 2**20
CHUNKS = 2


def split(x):
    high = x.astype(BF16)
    return high, (x - high.astype(F32)).astype(BF16)


def dot3(a, b, ca, cb):
    dims = (((ca,), (cb,)), ((), ()))
    dot = functools.partial(lax.dot_general, dimension_numbers=dims, preferred_element_type=F32)
    columns = b[0].shape[1 - cb]
    if columns <= 128:
        both = dot(a[0], jnp.concatenate([b[0], b[1]], axis=1 - cb))
        return both[:, :columns] + (both[:, columns:] + dot(a[1], b[0]))
    left = jnp.concatenate([a[0], a[0], a[1]], axis=ca)
    right = jnp.concatenate([b[0], b[1], b[0]], axis=cb)
    return dot(left, right)


def thirds(rows):
    zeros = jnp.zeros((16 - rows.shape[0], rows.shape[1]), F32)
    pieces = []
    for _ in range(3):
        piece = rows.astype(BF16)
        rows = rows - piece.astype(F32)
        pieces.append(jnp.concatenate([piece.astype(F32), zeros], axis=0))
    return jnp.concatenate(pieces, axis=0).astype(BF16)


def kernel(
    n, nh,
    x_hbm, step_hbm, log_hbm, b_hbm, c_hbm, g_hbm,
    out_ref, gin_ref, gstep_ref, wg_ref, rg_ref,
    x_ref, step_ref, log_ref, b_ref, c_ref, g_ref,
    st, r1, tz, zbuf, fsend, fs, tot, rs, wsum, back,
    in_sem, s1_send, s1_recv, z_send, z_recv, s3_send, s3_recv, h_send, h_recv,
):
    tokens, channels = x_ref.shape
    heads = step_ref.shape[0]
    width = channels // heads
    state = b_ref.shape[1]
    half = channels // 2
    m = n // 2
    ck = tokens // nh
    piece = state // CHUNKS

    ctx, head = lax.axis_index("ctx"), lax.axis_index("head")
    side, row = lax.rem(ctx, 2), lax.div(ctx, 2)
    partner = row * 2 + (1 - side)

    barrier = pltpu.get_barrier_semaphore()
    pl.semaphore_signal(barrier, inc=1, device_id=(partner, head), device_id_type=MESH)
    for k in range(1, m):
        peer = lax.rem(row + k, m) * 2 + side
        pl.semaphore_signal(barrier, inc=1, device_id=(peer, head), device_id_type=MESH)
    for k in range(1, nh):
        pl.semaphore_signal(
            barrier, inc=1, device_id=(ctx, lax.rem(head + k, nh)), device_id_type=MESH
        )

    loads = [
        pltpu.make_async_copy(source, target, in_sem.at[i])
        for i, (source, target) in enumerate((
            (log_hbm, log_ref), (step_hbm, step_ref), (b_hbm, b_ref),
            (c_hbm, c_ref), (x_hbm, x_ref), (g_hbm, g_ref),
        ))
    ]
    for load in loads:
        load.start()

    mid = tokens // 2
    row_ids = lax.broadcasted_iota(jnp.int32, (tokens, tokens), 0)
    col_ids = lax.broadcasted_iota(jnp.int32, (tokens, tokens), 1)
    weights = jnp.where(
        (row_ids <= col_ids) & (row_ids >= mid),
        1.0,
        jnp.where((row_ids > col_ids) & (row_ids < mid), -1.0, 0.0),
    ).astype(BF16)
    pick_row = lax.broadcasted_iota(jnp.int32, (48, 3 * channels), 0) % 16
    pick_col = lax.broadcasted_iota(jnp.int32, (48, 3 * channels), 1) // width
    expand = jnp.where(pick_row == pick_col, 1.0, 0.0).astype(BF16)

    loads[0].wait()
    logs = log_ref[...]
    sums = jnp.dot(thirds(logs), weights, preferred_element_type=F32)
    rel = sums[:heads] + sums[16 : 16 + heads] + sums[32 : 32 + heads]
    before = jnp.sum(logs[:, :mid], axis=1, keepdims=True)
    last = rel[:, tokens - 1 : tokens]
    into = jnp.exp(rel + before)
    outof = jnp.exp(last - rel)
    loads[1].wait()
    factors = thirds(jnp.concatenate([step_ref[...], into, outof], axis=0))
    wide = lax.dot_general(
        factors, expand, (((0,), (0,)), ((), ())), preferred_element_type=F32
    )
    step_w = wide[:, :channels]
    into_w = wide[:, channels : 2 * channels]
    outof_w = wide[:, 2 * channels :]

    loads[2].wait()
    write, write_t = split(b_ref[...]), split(b_ref[...].T)
    loads[3].wait()
    read, read_t = split(c_ref[...]), split(c_ref[...].T)
    loads[4].wait()
    scaled = x_ref[...] * step_w
    outof_s = split(outof_w * scaled)
    fwd = dot3(write_t, outof_s, 1, 0)
    loads[5].wait()
    grads = g_ref[...]
    into_g = split(into_w * grads)
    bwd = dot3(read_t, into_g, 1, 0)
    decay_rows = jnp.broadcast_to(into_w[tokens - 1 : tokens], (PAD, channels))
    for j in range(2):
        for d, whole in enumerate((fwd, bwd)):
            st[j, d, :PAD] = decay_rows[:, j * half : (j + 1) * half]
            st[j, d, PAD:] = whole[:, j * half : (j + 1) * half]

    def span(i):
        return pl.ds(0, PAD + piece) if i == 0 else pl.ds(PAD + i * piece, piece)

    def spread(decay):
        return jnp.concatenate([decay] * (piece // PAD), axis=0)

    pl.semaphore_wait(barrier, 1 + (m - 1) + (nh - 1))
    first_copies = [
        pltpu.make_async_remote_copy(
            st.at[1 - side, :, span(i)], r1.at[:, span(i)], s1_send.at[i], s1_recv.at[i],
            device_id=(partner, head), device_id_type=MESH,
        )
        for i in range(CHUNKS)
    ]
    for copy in first_copies:
        copy.start()

    scaled_2, grads_2 = split(scaled), split(grads)
    panels = ((0, mid), (mid, tokens))

    def part(pair, rows, columns=slice(None)):
        return tuple(x[rows, columns] for x in pair)

    inner = [
        dot3(part(read, slice(lo, hi)), part(write_t, slice(None), slice(0, hi)), 1, 0)
        for lo, hi in panels
    ]
    lanes = 2 * width
    lane = lax.broadcasted_iota(jnp.int32, (1, lanes), 1) // width
    rel_cols = jnp.concatenate([rel] * (8 // heads), axis=0).T
    out_ref[...] = jnp.zeros_like(out_ref)
    back[...] = jnp.zeros_like(back)
    wsum[...] = jnp.zeros_like(wsum)

    def near(h):
        here = slice(h // 2 * lanes, (h // 2 + 1) * lanes)
        mask = jnp.where(lane == h % 2, 1.0, 0.0).astype(BF16)
        scaled_h = tuple(x[:, here] * mask for x in scaled_2)
        grads_h = tuple(x[:, here] * mask for x in grads_2)
        for k, (lo, hi) in enumerate(panels):
            rows, reach = slice(lo, hi), slice(0, hi)
            gap = rel_cols[rows, h : h + 1] - rel[h : h + 1, reach]
            lower = row_ids[rows, reach] >= col_ids[rows, reach]
            decay = jnp.exp(jnp.where(lower, gap, -1e30))
            mixed = split(inner[k] * decay)
            out_ref[rows, here] += dot3(mixed, part(scaled_h, reach), 1, 0)
            back[reach, here] += dot3(mixed, part(grads_h, rows), 0, 0)
            wsum[rows, reach] += decay * dot3(
                part(grads_2, rows, here), part(scaled_h, reach), 1, 1
            )

    is_first = side == 0

    def rows_of(i):
        return slice(PAD + i * piece, PAD + (i + 1) * piece)

    def pair_parts(i):
        own, other = st[side, :, rows_of(i)], r1[:, rows_of(i)]
        own_decay, other_decay = st[side, 0, :PAD], r1[0, :PAD]
        return (
            jnp.where(is_first, own, other),
            jnp.where(is_first, other, own),
            spread(jnp.where(is_first, own_decay, other_decay)),
            spread(jnp.where(is_first, other_decay, own_decay)),
        )

    z_copies = []

    def send_totals(i):
        first_copies[i].wait()
        part_0, part_1, decay_0, decay_1 = pair_parts(i)
        tz[0, rows_of(i)] = decay_1 * part_0[0] + part_1[0]
        tz[1, rows_of(i)] = part_0[1] + decay_0 * part_1[1]
        if i == 0:
            for d in range(2):
                tz[d, :PAD] = decay_0[:PAD] * decay_1[:PAD]
        for k in range(1, m):
            peer_row = lax.rem(row + k, m)
            direction = jnp.where(peer_row > row, 0, 1)
            copy = pltpu.make_async_remote_copy(
                tz.at[direction, span(i)], zbuf.at[row, span(i)],
                z_send.at[i, k - 1], z_recv.at[i, row],
                device_id=(peer_row * 2 + side, head), device_id_type=MESH,
            )
            copy.start()
            z_copies.append(copy)

    last_copies = []

    def send_entering(i):
        def joined(j, carried):
            pltpu.make_async_remote_copy(
                tz.at[0, span(i)], zbuf.at[j, span(i)], z_send.at[i, 0], z_recv.at[i, j],
                device_id=(partner, head), device_id_type=MESH,
            ).wait_recv()
            return zbuf[j, rows_of(i)] + spread(zbuf[j, :PAD]) * carried

        zero = jnp.zeros((piece, half), F32)
        carry_f = lax.fori_loop(0, row, joined, zero)
        carry_b = lax.fori_loop(0, m - 1 - row, lambda k, c: joined(m - 1 - k, c), zero)
        part_0, part_1, decay_0, decay_1 = pair_parts(i)
        enter_f = (carry_f, decay_0 * carry_f + part_0[0])
        enter_b = (part_1[1] + decay_1 * carry_b, carry_b)
        for d, pair in enumerate((enter_f, enter_b)):
            fs[side, d, i * piece : (i + 1) * piece] = jnp.where(is_first, pair[0], pair[1])
            fsend[d, i * piece : (i + 1) * piece] = jnp.where(is_first, pair[1], pair[0])
        here = pl.ds(i * piece, piece)
        copy = pltpu.make_async_remote_copy(
            fsend.at[:, here], fs.at[side, :, here], s3_send.at[i], s3_recv.at[i],
            device_id=(partner, head), device_id_type=MESH,
        )
        copy.start()
        last_copies.append(copy)

    near(0)
    send_totals(0)
    near(1)
    send_totals(1)
    near(2)
    near(3)
    send_entering(0)
    mixed_sums = split(wsum[...])
    read_near = dot3(mixed_sums, write, 1, 0)
    write_near = dot3(mixed_sums, read, 0, 0)
    send_entering(1)
    for copy in last_copies:
        copy.wait()

    state_b = split(jnp.concatenate([fs[0, 1], fs[1, 1]], axis=1))
    state_f = split(jnp.concatenate([fs[0, 0], fs[1, 0]], axis=1))
    h_copies = []
    for which, (nearby, factor, far) in enumerate((
        (write_near, outof_s, state_b), (read_near, into_g, state_f),
    )):
        total = nearby + dot3(factor, far, 1, 1)
        for j in range(nh):
            tot[which, j] = total[j * ck : (j + 1) * ck]
        for k in range(1, nh):
            peer = lax.rem(head + k, nh)
            copy = pltpu.make_async_remote_copy(
                tot.at[which, peer], rs.at[which, k - 1],
                h_send.at[which, k - 1], h_recv.at[which, k - 1],
                device_id=(ctx, peer), device_id_type=MESH,
            )
            copy.start()
            h_copies.append(copy)

    out_ref[...] += into_w * dot3(read, state_f, 1, 0)
    back_all = back[...] + outof_w * dot3(write, state_b, 1, 0)
    gin_ref[...] = step_w * back_all
    pick_row = lax.broadcasted_iota(jnp.int32, (16, channels), 0)
    pick_col = lax.broadcasted_iota(jnp.int32, (16, channels), 1) // width
    pick = jnp.where(pick_row == pick_col, 1.0, 0.0).astype(BF16)
    high, low = split(x_ref[...] * back_all)
    nt = (((1,), (1,)), ((), ()))
    steps = lax.dot_general(pick, high, nt, preferred_element_type=F32) + lax.dot_general(
        pick, low, nt, preferred_element_type=F32
    )
    gstep_ref[...] = steps[:heads]

    for which, target in enumerate((wg_ref, rg_ref)):
        result = tot[which, head]
        for k in range(1, nh):
            h_copies[which * (nh - 1) + k - 1].wait()
            result = result + rs[which, k - 1]
        target[...] = result
    for copy in z_copies:
        copy.wait_send()


def place(*refs):
    count = len(refs) // 2
    sems = refs[-1]
    copies = [
        pltpu.make_async_copy(refs[i], refs[count + i], sems.at[i]) for i in range(count)
    ]
    for copy in copies:
        copy.start()
    for copy in copies:
        copy.wait()


def solution(mesh):
    n, nh = mesh.shape["ctx"], mesh.shape["head"]
    m = n // 2

    def shards(head_input, step_size, log_decay, write_proj, read_proj, grad_out):
        tokens, channels = head_input.shape
        heads = step_size.shape[0]
        state = write_proj.shape[1]
        half, ck = channels // 2, tokens // nh
        vmem = pl.BlockSpec(memory_space=pltpu.VMEM)
        hbm = pl.BlockSpec(memory_space=pltpu.HBM)
        dma = pltpu.SemaphoreType.DMA
        shapes = (
            jax.ShapeDtypeStruct((tokens, channels), F32),
            jax.ShapeDtypeStruct((tokens, channels), F32),
            jax.ShapeDtypeStruct((heads, tokens), F32),
            jax.ShapeDtypeStruct((ck, state), F32),
            jax.ShapeDtypeStruct((ck, state), F32),
        )
        results = pl.pallas_call(
            functools.partial(kernel, n, nh),
            out_shape=tuple(pltpu.VMEM(shape.shape, F32) for shape in shapes),
            in_specs=[hbm] * 6,
            out_specs=(vmem,) * 5,
            scratch_shapes=[
                pltpu.VMEM((tokens, channels), F32),
                pltpu.VMEM((heads, tokens), F32),
                pltpu.VMEM((heads, tokens), F32),
                pltpu.VMEM((tokens, state), F32),
                pltpu.VMEM((tokens, state), F32),
                pltpu.VMEM((tokens, channels), F32),
                pltpu.VMEM((2, 2, state + PAD, half), F32),
                pltpu.VMEM((2, state + PAD, half), F32),
                pltpu.VMEM((2, state + PAD, half), F32),
                pltpu.VMEM((m, state + PAD, half), F32),
                pltpu.VMEM((2, state, half), F32),
                pltpu.VMEM((2, 2, state, half), F32),
                pltpu.VMEM((2, nh, ck, state), F32),
                pltpu.VMEM((2, nh - 1, ck, state), F32),
                pltpu.VMEM((tokens, tokens), F32),
                pltpu.VMEM((tokens, channels), F32),
                dma((6,)),
                dma((CHUNKS,)), dma((CHUNKS,)),
                dma((CHUNKS, m - 1)), dma((CHUNKS, m)),
                dma((CHUNKS,)), dma((CHUNKS,)),
                dma((2, nh - 1)), dma((2, nh - 1)),
            ],
            compiler_params=pltpu.CompilerParams(
                collective_id=0, has_side_effects=True, vmem_limit_bytes=GRANT
            ),
        )(*(
            pltpu.with_memory_space_constraint(x, pltpu.HBM)
            for x in (head_input, step_size, log_decay, write_proj, read_proj, grad_out)
        ))
        return pl.pallas_call(
            place,
            out_shape=shapes,
            in_specs=[vmem] * 5,
            out_specs=(hbm,) * 5,
            scratch_shapes=[dma((5,))],
            compiler_params=pltpu.CompilerParams(vmem_limit_bytes=4 * 2**20),
        )(*(pltpu.with_memory_space_constraint(x, pltpu.VMEM) for x in results))

    return jax.shard_map(
        shards,
        mesh=mesh,
        in_specs=(
            P("ctx", "head"), P("head", "ctx"), P("head", "ctx"),
            P("ctx", None), P("ctx", None), P("ctx", "head"),
        ),
        out_specs=(
            P("ctx", "head"), P("ctx", "head"), P("head", "ctx"),
            P(("ctx", "head"), None), P(("ctx", "head"), None),
        ),
        check_vma=False,
    )
```

```python
import functools

import jax
import jax.numpy as jnp
from jax import lax
from jax.experimental import pallas as pl
from jax.experimental.pallas import tpu as pltpu
from jax.sharding import PartitionSpec as P

MESH = pl.DeviceIdType.MESH
F32 = jnp.float32
BF16 = jnp.bfloat16
PAD = 8
GRANT = 32 * 2**20
CHUNKS = 2


def split(x):
    high = x.astype(BF16)
    return high, (x - high.astype(F32)).astype(BF16)


def dot3(a, b, ca, cb):
    dims = (((ca,), (cb,)), ((), ()))
    dot = functools.partial(lax.dot_general, dimension_numbers=dims, preferred_element_type=F32)
    columns = b[0].shape[1 - cb]
    if columns <= 128:
        both = dot(a[0], jnp.concatenate([b[0], b[1]], axis=1 - cb))
        return both[:, :columns] + (both[:, columns:] + dot(a[1], b[0]))
    left = jnp.concatenate([a[0], a[0], a[1]], axis=ca)
    right = jnp.concatenate([b[0], b[1], b[0]], axis=cb)
    return dot(left, right)


def thirds(rows):
    zeros = jnp.zeros((16 - rows.shape[0], rows.shape[1]), F32)
    pieces = []
    for _ in range(3):
        piece = rows.astype(BF16)
        rows = rows - piece.astype(F32)
        pieces.append(jnp.concatenate([piece.astype(F32), zeros], axis=0))
    return jnp.concatenate(pieces, axis=0).astype(BF16)


def kernel(
    n, nh,
    x_hbm, step_hbm, log_hbm, b_hbm, c_hbm, g_hbm,
    out_ref, gin_ref, gstep_ref, wg_ref, rg_ref,
    x_ref, step_ref, log_ref, b_ref, c_ref, g_ref,
    st, r1, tz, zbuf, fsend, fs, tot, rs, wsum, back,
    in_sem, s1_send, s1_recv, z_send, z_recv, s3_send, s3_recv, h_send, h_recv,
):
    tokens, channels = x_ref.shape
    heads = step_ref.shape[0]
    width = channels // heads
    state = b_ref.shape[1]
    half = channels // 2
    m = n // 2
    ck = tokens // nh
    piece = state // CHUNKS

    ctx, head = lax.axis_index("ctx"), lax.axis_index("head")
    side, row = lax.rem(ctx, 2), lax.div(ctx, 2)
    partner = row * 2 + (1 - side)

    barrier = pltpu.get_barrier_semaphore()
    pl.semaphore_signal(barrier, inc=1, device_id=(partner, head), device_id_type=MESH)
    for k in range(1, m):
        peer = lax.rem(row + k, m) * 2 + side
        pl.semaphore_signal(barrier, inc=1, device_id=(peer, head), device_id_type=MESH)
    for k in range(1, nh):
        pl.semaphore_signal(
            barrier, inc=1, device_id=(ctx, lax.rem(head + k, nh)), device_id_type=MESH
        )

    loads = [
        pltpu.make_async_copy(source, target, in_sem.at[i])
        for i, (source, target) in enumerate((
            (log_hbm, log_ref), (step_hbm, step_ref), (b_hbm, b_ref),
            (x_hbm, x_ref), (c_hbm, c_ref), (g_hbm, g_ref),
        ))
    ]
    for load in loads:
        load.start()

    mid = tokens // 2
    row_ids = lax.broadcasted_iota(jnp.int32, (tokens, tokens), 0)
    col_ids = lax.broadcasted_iota(jnp.int32, (tokens, tokens), 1)
    weights = jnp.where(
        (row_ids <= col_ids) & (row_ids >= mid),
        1.0,
        jnp.where((row_ids > col_ids) & (row_ids < mid), -1.0, 0.0),
    ).astype(BF16)
    pick_row = lax.broadcasted_iota(jnp.int32, (48, 3 * channels), 0) % 16
    pick_col = lax.broadcasted_iota(jnp.int32, (48, 3 * channels), 1) // width
    expand = jnp.where(pick_row == pick_col, 1.0, 0.0).astype(BF16)

    loads[0].wait()
    logs = log_ref[...]
    sums = jnp.dot(thirds(logs), weights, preferred_element_type=F32)
    rel = sums[:heads] + sums[16 : 16 + heads] + sums[32 : 32 + heads]
    before = jnp.sum(logs[:, :mid], axis=1, keepdims=True)
    last = rel[:, tokens - 1 : tokens]
    into = jnp.exp(rel + before)
    outof = jnp.exp(last - rel)
    loads[1].wait()
    factors = thirds(jnp.concatenate([step_ref[...], into, outof], axis=0))
    wide = lax.dot_general(
        factors, expand, (((0,), (0,)), ((), ())), preferred_element_type=F32
    )
    step_w = wide[:, :channels]
    into_w = wide[:, channels : 2 * channels]
    outof_w = wide[:, 2 * channels :]

    loads[2].wait()
    write, write_t = split(b_ref[...]), split(b_ref[...].T)
    decay_rows = jnp.broadcast_to(into_w[tokens - 1 : tokens], (PAD, channels))

    def span(i):
        return pl.ds(0, PAD + piece) if i == 0 else pl.ds(PAD + i * piece, piece)

    def spread(decay):
        return jnp.concatenate([decay] * (piece // PAD), axis=0)

    def send_first(d, whole):
        for j in range(2):
            st[j, d, :PAD] = decay_rows[:, j * half : (j + 1) * half]
            st[j, d, PAD:] = whole[:, j * half : (j + 1) * half]
        copies = [
            pltpu.make_async_remote_copy(
                st.at[1 - side, d, span(i)], r1.at[d, span(i)],
                s1_send.at[d, i], s1_recv.at[d, i],
                device_id=(partner, head), device_id_type=MESH,
            )
            for i in range(CHUNKS)
        ]
        for copy in copies:
            copy.start()
        return copies

    loads[3].wait()
    scaled = x_ref[...] * step_w
    outof_s = split(outof_w * scaled)
    fwd = dot3(write_t, outof_s, 1, 0)
    pl.semaphore_wait(barrier, 1 + (m - 1) + (nh - 1))
    fwd_copies = send_first(0, fwd)
    loads[4].wait()
    read, read_t = split(c_ref[...]), split(c_ref[...].T)
    loads[5].wait()
    grads = g_ref[...]
    into_g = split(into_w * grads)
    bwd_copies = send_first(1, dot3(read_t, into_g, 1, 0))

    scaled_2, grads_2 = split(scaled), split(grads)
    panels = ((0, mid), (mid, tokens))

    def part(pair, rows, columns=slice(None)):
        return tuple(x[rows, columns] for x in pair)

    inner = [
        dot3(part(read, slice(lo, hi)), part(write_t, slice(None), slice(0, hi)), 1, 0)
        for lo, hi in panels
    ]
    lanes = 2 * width
    lane = lax.broadcasted_iota(jnp.int32, (1, lanes), 1) // width
    rel_cols = jnp.concatenate([rel] * (8 // heads), axis=0).T
    out_ref[...] = jnp.zeros_like(out_ref)
    back[...] = jnp.zeros_like(back)
    wsum[...] = jnp.zeros_like(wsum)

    def near(h):
        here = slice(h // 2 * lanes, (h // 2 + 1) * lanes)
        mask = jnp.where(lane == h % 2, 1.0, 0.0).astype(BF16)
        scaled_h = tuple(x[:, here] * mask for x in scaled_2)
        grads_h = tuple(x[:, here] * mask for x in grads_2)
        for k, (lo, hi) in enumerate(panels):
            rows, reach = slice(lo, hi), slice(0, hi)
            gap = rel_cols[rows, h : h + 1] - rel[h : h + 1, reach]
            lower = row_ids[rows, reach] >= col_ids[rows, reach]
            decay = jnp.exp(jnp.where(lower, gap, -1e30))
            mixed = split(inner[k] * decay)
            out_ref[rows, here] += dot3(mixed, part(scaled_h, reach), 1, 0)
            back[reach, here] += dot3(mixed, part(grads_h, rows), 0, 0)
            wsum[rows, reach] += decay * dot3(
                part(grads_2, rows, here), part(scaled_h, reach), 1, 1
            )

    is_first = side == 0

    def rows_of(i):
        return slice(PAD + i * piece, PAD + (i + 1) * piece)

    def pair_parts(i):
        own, other = st[side, :, rows_of(i)], r1[:, rows_of(i)]
        own_decay, other_decay = st[side, 0, :PAD], r1[0, :PAD]
        return (
            jnp.where(is_first, own, other),
            jnp.where(is_first, other, own),
            spread(jnp.where(is_first, own_decay, other_decay)),
            spread(jnp.where(is_first, other_decay, own_decay)),
        )

    z_copies = []

    def send_totals(i):
        fwd_copies[i].wait()
        bwd_copies[i].wait()
        part_0, part_1, decay_0, decay_1 = pair_parts(i)
        tz[0, rows_of(i)] = decay_1 * part_0[0] + part_1[0]
        tz[1, rows_of(i)] = part_0[1] + decay_0 * part_1[1]
        if i == 0:
            for d in range(2):
                tz[d, :PAD] = decay_0[:PAD] * decay_1[:PAD]
        for k in range(1, m):
            peer_row = lax.rem(row + k, m)
            direction = jnp.where(peer_row > row, 0, 1)
            copy = pltpu.make_async_remote_copy(
                tz.at[direction, span(i)], zbuf.at[row, span(i)],
                z_send.at[i, k - 1], z_recv.at[i, row],
                device_id=(peer_row * 2 + side, head), device_id_type=MESH,
            )
            copy.start()
            z_copies.append(copy)

    last_copies = []

    def send_entering(i):
        def joined(j, carried):
            pltpu.make_async_remote_copy(
                tz.at[0, span(i)], zbuf.at[j, span(i)], z_send.at[i, 0], z_recv.at[i, j],
                device_id=(partner, head), device_id_type=MESH,
            ).wait_recv()
            return zbuf[j, rows_of(i)] + spread(zbuf[j, :PAD]) * carried

        zero = jnp.zeros((piece, half), F32)
        carry_f = lax.fori_loop(0, row, joined, zero)
        carry_b = lax.fori_loop(0, m - 1 - row, lambda k, c: joined(m - 1 - k, c), zero)
        part_0, part_1, decay_0, decay_1 = pair_parts(i)
        enter_f = (carry_f, decay_0 * carry_f + part_0[0])
        enter_b = (part_1[1] + decay_1 * carry_b, carry_b)
        for d, pair in enumerate((enter_f, enter_b)):
            fs[side, d, i * piece : (i + 1) * piece] = jnp.where(is_first, pair[0], pair[1])
            fsend[d, i * piece : (i + 1) * piece] = jnp.where(is_first, pair[1], pair[0])
        here = pl.ds(i * piece, piece)
        copy = pltpu.make_async_remote_copy(
            fsend.at[:, here], fs.at[side, :, here], s3_send.at[i], s3_recv.at[i],
            device_id=(partner, head), device_id_type=MESH,
        )
        copy.start()
        last_copies.append(copy)

    near(0)
    send_totals(0)
    near(1)
    send_totals(1)
    near(2)
    near(3)
    send_entering(0)
    mixed_sums = split(wsum[...])
    read_near = dot3(mixed_sums, write, 1, 0)
    write_near = dot3(mixed_sums, read, 0, 0)
    send_entering(1)
    for copy in last_copies:
        copy.wait()

    state_b = split(jnp.concatenate([fs[0, 1], fs[1, 1]], axis=1))
    state_f = split(jnp.concatenate([fs[0, 0], fs[1, 0]], axis=1))
    h_copies = []
    for which, (nearby, factor, far) in enumerate((
        (write_near, outof_s, state_b), (read_near, into_g, state_f),
    )):
        total = nearby + dot3(factor, far, 1, 1)
        for j in range(nh):
            tot[which, j] = total[j * ck : (j + 1) * ck]
        for k in range(1, nh):
            peer = lax.rem(head + k, nh)
            copy = pltpu.make_async_remote_copy(
                tot.at[which, peer], rs.at[which, k - 1],
                h_send.at[which, k - 1], h_recv.at[which, k - 1],
                device_id=(ctx, peer), device_id_type=MESH,
            )
            copy.start()
            h_copies.append(copy)

    out_ref[...] += into_w * dot3(read, state_f, 1, 0)
    back_all = back[...] + outof_w * dot3(write, state_b, 1, 0)
    gin_ref[...] = step_w * back_all
    pick_row = lax.broadcasted_iota(jnp.int32, (16, channels), 0)
    pick_col = lax.broadcasted_iota(jnp.int32, (16, channels), 1) // width
    pick = jnp.where(pick_row == pick_col, 1.0, 0.0).astype(BF16)
    high, low = split(x_ref[...] * back_all)
    nt = (((1,), (1,)), ((), ()))
    steps = lax.dot_general(pick, high, nt, preferred_element_type=F32) + lax.dot_general(
        pick, low, nt, preferred_element_type=F32
    )
    gstep_ref[...] = steps[:heads]

    for which, target in enumerate((wg_ref, rg_ref)):
        result = tot[which, head]
        for k in range(1, nh):
            h_copies[which * (nh - 1) + k - 1].wait()
            result = result + rs[which, k - 1]
        target[...] = result
    for copy in z_copies:
        copy.wait_send()


def place(*refs):
    count = len(refs) // 2
    sems = refs[-1]
    copies = [
        pltpu.make_async_copy(refs[i], refs[count + i], sems.at[i]) for i in range(count)
    ]
    for copy in copies:
        copy.start()
    for copy in copies:
        copy.wait()


def solution(mesh):
    n, nh = mesh.shape["ctx"], mesh.shape["head"]
    m = n // 2

    def shards(head_input, step_size, log_decay, write_proj, read_proj, grad_out):
        tokens, channels = head_input.shape
        heads = step_size.shape[0]
        state = write_proj.shape[1]
        half, ck = channels // 2, tokens // nh
        vmem = pl.BlockSpec(memory_space=pltpu.VMEM)
        hbm = pl.BlockSpec(memory_space=pltpu.HBM)
        dma = pltpu.SemaphoreType.DMA
        shapes = (
            jax.ShapeDtypeStruct((tokens, channels), F32),
            jax.ShapeDtypeStruct((tokens, channels), F32),
            jax.ShapeDtypeStruct((heads, tokens), F32),
            jax.ShapeDtypeStruct((ck, state), F32),
            jax.ShapeDtypeStruct((ck, state), F32),
        )
        results = pl.pallas_call(
            functools.partial(kernel, n, nh),
            out_shape=tuple(pltpu.VMEM(shape.shape, F32) for shape in shapes),
            in_specs=[hbm] * 6,
            out_specs=(vmem,) * 5,
            scratch_shapes=[
                pltpu.VMEM((tokens, channels), F32),
                pltpu.VMEM((heads, tokens), F32),
                pltpu.VMEM((heads, tokens), F32),
                pltpu.VMEM((tokens, state), F32),
                pltpu.VMEM((tokens, state), F32),
                pltpu.VMEM((tokens, channels), F32),
                pltpu.VMEM((2, 2, state + PAD, half), F32),
                pltpu.VMEM((2, state + PAD, half), F32),
                pltpu.VMEM((2, state + PAD, half), F32),
                pltpu.VMEM((m, state + PAD, half), F32),
                pltpu.VMEM((2, state, half), F32),
                pltpu.VMEM((2, 2, state, half), F32),
                pltpu.VMEM((2, nh, ck, state), F32),
                pltpu.VMEM((2, nh - 1, ck, state), F32),
                pltpu.VMEM((tokens, tokens), F32),
                pltpu.VMEM((tokens, channels), F32),
                dma((6,)),
                dma((2, CHUNKS)), dma((2, CHUNKS)),
                dma((CHUNKS, m - 1)), dma((CHUNKS, m)),
                dma((CHUNKS,)), dma((CHUNKS,)),
                dma((2, nh - 1)), dma((2, nh - 1)),
            ],
            compiler_params=pltpu.CompilerParams(
                collective_id=0, has_side_effects=True, vmem_limit_bytes=GRANT
            ),
        )(*(
            pltpu.with_memory_space_constraint(x, pltpu.HBM)
            for x in (head_input, step_size, log_decay, write_proj, read_proj, grad_out)
        ))
        return pl.pallas_call(
            place,
            out_shape=shapes,
            in_specs=[vmem] * 5,
            out_specs=(hbm,) * 5,
            scratch_shapes=[dma((5,))],
            compiler_params=pltpu.CompilerParams(vmem_limit_bytes=4 * 2**20),
        )(*(pltpu.with_memory_space_constraint(x, pltpu.VMEM) for x in results))

    return jax.shard_map(
        shards,
        mesh=mesh,
        in_specs=(
            P("ctx", "head"), P("head", "ctx"), P("head", "ctx"),
            P("ctx", None), P("ctx", None), P("ctx", "head"),
        ),
        out_specs=(
            P("ctx", "head"), P("ctx", "head"), P("head", "ctx"),
            P(("ctx", "head"), None), P(("ctx", "head"), None),
        ),
        check_vma=False,
    )
```
